32 devices in a mesh: band: 4 (over y, x), tile: 8 (over z, core).
Axes of the slice: x: 2, y: 2, z: 4, core: 2. Of those that a mesh axis runs over, the one named last changes fastest.
Arguments:
- winds: float32 [2, 8, 48, 64, 720], P(None, None, 'band', 'tile'), may hold values from -8 to 8
- basis: bfloat16 [24, 48, 2, 64, 720], P(None, 'band', None, 'tile'), may hold values from -48 to 48
- ground: int32 [64, 720], P('tile'), may hold values from 24 to 48
Outputs:
- new_basis: float32 [24, 48, 2, 64, 720], P(None, 'band', None, 'tile')
The draws below stay inside these ranges and needn't reach their ends.
All inputs are finite; a program needn't handle non-finite values.
Results may differ from the reference program's by a relative error of at most 0.0015.
Values sent between devices are 32-bit elements; how exact they have to be, the bound alone decides.
No kernel may reach another device: no remote copies, remote signals or barrier semaphores. Data moves between devices by JAX's collectives and lax.ppermute only.
A program may use at most 128 MiB of HBM per device.

```python
import math
import jax
import jax.numpy as jnp
from jax import lax

K = 24
SNAP = 8
ITERS = 4
LAT = 720
LEVELS = 48
NLON = 64
COLS = 32


def lat_diff_drawn(field):
    ext = jnp.pad(field, [(0, 0)] * (field.ndim - 1) + [(2, 2)])
    return (8.0 * (ext[..., 3:-1] - ext[..., 1:-3]) - (ext[..., 4:] - ext[..., :-4])) / 12.0


def lon_diff_drawn(field):
    return (8.0 * (jnp.roll(field, -1, -2) - jnp.roll(field, 1, -2)) - (jnp.roll(field, -2, -2) - jnp.roll(field, 2, -2))) / 12.0


def shared_modes(key):
    mode_key = jax.random.fold_in(key, 101)
    shape = (6, 2, LEVELS, NLON, LAT)
    return jax.random.truncated_normal(mode_key, -6.0, 6.0, shape, jnp.float32)


def mode_fields(modes):
    cosine = jnp.cos((jnp.arange(LAT, dtype=jnp.float32) + 0.5) * (jnp.pi / LAT) - jnp.pi / 2)
    spread = 0.9 * (2.0 / math.pi * math.log(4.0 * LAT / math.pi) + 0.64)
    east_wind = modes[:, 0]
    north_wind = modes[:, 1]
    vorticity = (lon_diff_drawn(north_wind) - lat_diff_drawn(east_wind * cosine)) / cosine
    divergence = (lon_diff_drawn(east_wind) + lat_diff_drawn(north_wind * cosine)) / cosine
    return jnp.stack([vorticity, divergence], axis=2) * (jnp.sqrt(cosine) / math.sqrt(spread))


def draw_winds(key, part):
    modes = shared_modes(key)
    noise_key = jax.random.fold_in(key, 202)
    loading_key = jax.random.fold_in(key, 303)
    shape = (2, SNAP, LEVELS, NLON, LAT)
    winds = 0.8 * jax.random.truncated_normal(noise_key, -6.0, 6.0, shape, jnp.float32)
    loading = 0.5 * jax.random.normal(loading_key, (SNAP, 6), jnp.float32)
    for mode_id in range(6):
        winds = winds + loading[:, mode_id][None, :, None, None, None] * modes[mode_id][:, None]
    return jnp.clip(winds, -8.0, 8.0)


def draw_basis(key, part):
    fields = mode_fields(shared_modes(key))
    noise_key = jax.random.fold_in(key, 404)
    mixing_key = jax.random.fold_in(key, 505)
    shape = (K, LEVELS, 2, NLON, LAT)
    steps_k = jnp.arange(K, dtype=jnp.float32)
    basis = jax.random.truncated_normal(noise_key, -6.0, 6.0, shape, jnp.float32)
    mixing = 0.4 * jax.random.normal(mixing_key, (K, 6), jnp.float32)
    scales = 2.0 * jnp.power(0.97, steps_k)
    for mode_id in range(6):
        basis = basis + mixing[:, mode_id][:, None, None, None, None] * fields[mode_id][None]
    return jnp.clip(basis * scales[:, None, None, None, None], -48.0, 48.0).astype(jnp.bfloat16)


def touch_ends(array, own_key, least, top_value):
    index_at = [jax.random.randint(jax.random.fold_in(own_key, axis), (), 0, length) for axis, length in enumerate(array.shape)]
    widest = array.shape.index(max(array.shape))
    next_to = index_at[:widest] + [(index_at[widest] + 1) % array.shape[widest]] + index_at[widest + 1:]
    return array.at[tuple(index_at)].set(least).at[tuple(next_to)].set(top_value)


def setup_inputs(seed: int = 0) -> dict:
    streams_of = jax.random.split(jax.random.key(seed), 4)
    return {
        "winds": draw_winds(jax.random.fold_in(streams_of[3], 71), 0),
        "basis": draw_basis(jax.random.fold_in(streams_of[3], 71), 0),
        "ground": touch_ends(jax.random.randint(streams_of[2], (NLON, LAT), LEVELS // 2, LEVELS + 1), jax.random.fold_in(streams_of[2], 1), LEVELS // 2, LEVELS).astype(jnp.int32),
    }


HIGH = lax.Precision.HIGHEST

def lat_diff(field):
    ext = jnp.pad(field, [(0, 0)] * (field.ndim - 1) + [(2, 2)])
    return (8.0 * (ext[..., 3:-1] - ext[..., 1:-3]) - (ext[..., 4:] - ext[..., :-4])) / 12.0

def lon_diff(field):
    return (8.0 * (jnp.roll(field, -1, -2) - jnp.roll(field, 1, -2)) - (jnp.roll(field, -2, -2) - jnp.roll(field, 2, -2))) / 12.0

def orthonormal(block):

    def one_column(col_id, ortho):
        column = lax.dynamic_index_in_dim(block, col_id, 1, keepdims=False)
        for repeat in range(2):
            column = column - jnp.dot(ortho, jnp.dot(column, ortho, precision=HIGH), precision=HIGH)
        column = column / jnp.sqrt(jnp.dot(column, column, precision=HIGH))
        return lax.dynamic_update_index_in_dim(ortho, column, col_id, 1)
    return lax.fori_loop(0, block.shape[1], one_column, jnp.zeros_like(block))

def reference(winds, basis, ground):
    cosine = jnp.cos((jnp.arange(LAT, dtype=jnp.float32) + 0.5) * (jnp.pi / LAT) - jnp.pi / 2)
    weight = jnp.sqrt(cosine)

    def stacked_level(level_id):
        wind_level = lax.dynamic_index_in_dim(winds, level_id, 2, keepdims=False)
        basis_level = lax.dynamic_index_in_dim(basis, level_id, 1, keepdims=False)
        east_wind, north_wind = (wind_level[0], wind_level[1])
        vorticity = (lon_diff(north_wind) - lat_diff(east_wind * cosine)) / cosine
        divergence = (lon_diff(east_wind) + lat_diff(north_wind * cosine)) / cosine
        inside_air = (level_id < ground).astype(jnp.float32)
        snapshot_cols = (jnp.stack([vorticity, divergence], axis=1) * (weight * inside_air)).astype(jnp.bfloat16)
        stacked = jnp.concatenate([basis_level, snapshot_cols], axis=0)
        return stacked.reshape(stacked.shape[0], -1)
    level_ids = jnp.arange(LEVELS, dtype=jnp.int32)

    def add_level(total, level_id):
        stacked = stacked_level(level_id)
        return (total + jnp.dot(stacked, stacked.T, preferred_element_type=jnp.float32), None)
    gram, _ = lax.scan(add_level, jnp.zeros((COLS, COLS), jnp.float32), level_ids)
    frame = jnp.eye(COLS, K, dtype=jnp.float32)
    for sweep in range(ITERS):
        frame = orthonormal(jnp.dot(gram, frame, precision=HIGH))

    def project(level_id):
        stacked = stacked_level(level_id).astype(jnp.float32)
        return jnp.dot(frame.T, stacked, precision=HIGH).reshape(K, 2, NLON, LAT)
    result = lax.map(project, level_ids)
    return jnp.transpose(result, (1, 0, 2, 3, 4))
```

```python
import jax
import jax.numpy as jnp
from jax import lax
from jax.experimental import pallas as pl
from jax.experimental.pallas import tpu as pltpu
from jax.sharding import PartitionSpec as P

ITERS = 4
HIGH = lax.Precision.HIGHEST
LON = 8
GROUP = 4
MIB = 1 << 20
F32 = jnp.float32
BF16 = jnp.bfloat16


def rows_of(shape):
    return lax.broadcasted_iota(jnp.int32, shape, len(shape) - 2)


def lanes_of(shape):
    return lax.broadcasted_iota(jnp.int32, shape, len(shape) - 1)


def gather_rows(planes, first):
    row = rows_of(planes[0].shape)
    out = None
    for i in reversed(range(GROUP)):
        shift = (2 * i - first) % LON
        moved = pltpu.roll(planes[i], shift, 0) if shift else planes[i]
        out = moved if out is None else jnp.where(row < 2 * (i + 1), moved, out)
    return out


def pack_kernel(winds, up, down):
    fields, _, levels = winds.shape[:3]
    for f in range(fields):
        for g in range(levels // GROUP):
            planes = [winds[f, 0, g * GROUP + i] for i in range(GROUP)]
            up[f, 0, g] = gather_rows(planes, LON - 2)
            down[f, 0, g] = gather_rows(planes, 0)


def pack(winds):
    fields, snaps, levels, lon, lat = winds.shape
    groups = levels // GROUP
    out = jax.ShapeDtypeStruct((fields, snaps, groups, lon, lat), F32)
    spec = pl.BlockSpec((fields, 1, groups, lon, lat), lambda t: (0, t, 0, 0, 0))
    return pl.pallas_call(
        pack_kernel,
        grid=(snaps,),
        in_specs=[pl.BlockSpec((fields, 1, levels, lon, lat), lambda t: (0, t, 0, 0, 0))],
        out_specs=[spec, spec],
        out_shape=[out, out],
        compiler_params=pltpu.CompilerParams(vmem_limit_bytes=32 * MIB),
        name="pack_halo",
    )(winds)


def lat_diff(x):
    lat = x.shape[1]
    wide = pl.cdiv(lat + 2, 128) * 128
    x = jnp.concatenate([x, jnp.zeros((LON, wide - lat), F32)], axis=1)
    near = pltpu.roll(x, wide - 1, 1) - pltpu.roll(x, 1, 1)
    far = pltpu.roll(x, wide - 2, 1) - pltpu.roll(x, 2, 1)
    return (8.0 * near - far)[:, :lat]


def lon_diff_inside(x):
    row = rows_of(x.shape)
    out = jnp.where(row < 7, 8.0 * pltpu.roll(x, 7, 0), 0.0)
    out = out - jnp.where(row > 0, 8.0 * pltpu.roll(x, 1, 0), 0.0)
    out = out - jnp.where(row < 6, pltpu.roll(x, 6, 0), 0.0)
    return out + jnp.where(row > 1, pltpu.roll(x, 2, 0), 0.0)


def same_lon(shape):
    return rows_of(shape) % LON == lanes_of(shape) % LON


def lon_trace(prod):
    rows, cols = prod.shape
    kept = jnp.where(same_lon(prod.shape), prod, 0.0)
    kept = jnp.sum(kept.reshape(rows // LON, LON, cols), axis=1)
    one = (rows_of((cols, cols // LON)) // LON == lanes_of((cols, cols // LON))).astype(F32)
    return jnp.dot(kept, one, precision=HIGH, preferred_element_type=F32)


def dot_lanes(a, b):
    return lax.dot_general(a, b, (((1,), (1,)), ((), ())), preferred_element_type=F32)


def local_kernel(winds, basis, ground, rows, partial, flat, gram, acc):
    level = pl.program_id(0)
    snaps, lat = winds.shape[1], winds.shape[4]
    rank = basis.shape[0]

    @pl.when(level == 0)
    def _():
        acc[...] = jnp.zeros_like(acc)

    cosine = jnp.broadcast_to(rows[0:1, :], (LON, lat))
    scale = jnp.where(level < ground[...], jnp.broadcast_to(rows[1:2, :], (LON, lat)), 0.0)
    for t in range(snaps):
        east, north = winds[0, t, 0], winds[1, t, 0]
        partial[0, 0, t] = (lon_diff_inside(north) - lat_diff(east * cosine)) * scale
        partial[0, 1, t] = (lon_diff_inside(east) + lat_diff(north * cosine)) * scale
    for f in range(2):
        block = basis[:, 0, f].astype(F32).reshape(rank * LON, lat).astype(BF16)
        flat[0, f] = block
        acc[...] += dot_lanes(block, block)

    @pl.when(level == pl.num_programs(0) - 1)
    def _():
        gram[...] = lon_trace(acc[...])


def local(winds, basis, ground, rows):
    fields, snaps, levels, lon, lat = winds.shape
    rank = basis.shape[0]
    return pl.pallas_call(
        local_kernel,
        grid=(levels,),
        in_specs=[
            pl.BlockSpec((fields, snaps, 1, lon, lat), lambda l: (0, 0, l, 0, 0)),
            pl.BlockSpec((rank, 1, fields, lon, lat), lambda l: (0, l, 0, 0, 0)),
            pl.BlockSpec((lon, lat), lambda l: (0, 0)),
            pl.BlockSpec((LON, lat), lambda l: (0, 0)),
        ],
        out_specs=[
            pl.BlockSpec((1, fields, snaps, lon, lat), lambda l: (l, 0, 0, 0, 0)),
            pl.BlockSpec((1, fields, rank * lon, lat), lambda l: (l, 0, 0, 0)),
            pl.BlockSpec((rank, rank), lambda l: (0, 0)),
        ],
        out_shape=[
            jax.ShapeDtypeStruct((levels, fields, snaps, lon, lat), F32),
            jax.ShapeDtypeStruct((levels, fields, rank * lon, lat), BF16),
            jax.ShapeDtypeStruct((rank, rank), F32),
        ],
        scratch_shapes=[pltpu.VMEM((rank * lon, rank * lon), F32)],
        compiler_params=pltpu.CompilerParams(vmem_limit_bytes=32 * MIB),
        cost_estimate=pl.CostEstimate(
            flops=2 * 10**9, bytes_accessed=26 * 10**6, transcendentals=0
        ),
        name="local_stencil",
    )(winds, basis, ground, rows)


def edge_kernel(partial, before, after, ground, rows, flat, gram_basis, snap, gram, acc_b, acc_s):
    level = pl.program_id(0)
    snaps, lat = partial.shape[2], partial.shape[4]
    rank = gram_basis.shape[0]

    @pl.when(level == 0)
    def _():
        acc_b[...] = jnp.zeros_like(acc_b)
        acc_s[...] = jnp.zeros_like(acc_s)

    scale = jnp.where(level < ground[...], jnp.broadcast_to(rows[1:2, :], (LON, lat)), 0.0)
    row = rows_of((LON, lat))
    place = 2 * lax.rem(level, GROUP)
    low = jnp.where(row == 0, -8.0 * scale, scale)
    high = jnp.where(row == 7, 8.0 * scale, -scale)
    for f in range(2):
        planes = []
        for t in range(snaps):
            b = pltpu.roll(before[1 - f, t, 0], LON - place, 0)
            a = pltpu.roll(after[1 - f, t, 0], LON - 2 - place, 0)
            near_b = jnp.where(row == 0, pltpu.roll(b, 7, 0), b)
            near_a = jnp.where(row == 7, pltpu.roll(a, 1, 0), a)
            edge = jnp.where(row < 2, near_b * low, jnp.where(row > 5, near_a * high, 0.0))
            far = jnp.where(row == 0, b * scale, jnp.where(row == 7, -a * scale, 0.0))
            planes.append(partial[0, f, t] + (edge + far))
        block = jnp.concatenate(planes, axis=0).astype(BF16)
        snap[0, f] = block
        acc_b[...] += dot_lanes(block, flat[0, f])
        acc_s[...] += dot_lanes(block, block)

    @pl.when(level == pl.num_programs(0) - 1)
    def _():
        cross = lon_trace(acc_b[...])
        gram[0:rank, 0:rank] = gram_basis[...]
        gram[rank:, 0:rank] = cross
        gram[rank:, rank:] = lon_trace(acc_s[...])
        gram[0:rank, rank:] = cross.T


def edges(partial, before, after, ground, rows, flat, gram_basis):
    levels, fields, snaps, lon, lat = partial.shape
    rank = gram_basis.shape[0]
    cols = rank + snaps
    halo = pl.BlockSpec((fields, snaps, 1, lon, lat), lambda l: (0, 0, l // GROUP, 0, 0))
    return pl.pallas_call(
        edge_kernel,
        grid=(levels,),
        in_specs=[
            pl.BlockSpec((1, fields, snaps, lon, lat), lambda l: (l, 0, 0, 0, 0)),
            halo,
            halo,
            pl.BlockSpec((lon, lat), lambda l: (0, 0)),
            pl.BlockSpec((LON, lat), lambda l: (0, 0)),
            pl.BlockSpec((1, fields, rank * lon, lat), lambda l: (l, 0, 0, 0)),
            pl.BlockSpec((rank, rank), lambda l: (0, 0)),
        ],
        out_specs=[
            pl.BlockSpec((1, fields, snaps * lon, lat), lambda l: (l, 0, 0, 0)),
            pl.BlockSpec((cols, cols), lambda l: (0, 0)),
        ],
        out_shape=[
            jax.ShapeDtypeStruct((levels, fields, snaps * lon, lat), BF16),
            jax.ShapeDtypeStruct((cols, cols), F32),
        ],
        scratch_shapes=[
            pltpu.VMEM((snaps * lon, rank * lon), F32),
            pltpu.VMEM((snaps * lon, snaps * lon), F32),
        ],
        compiler_params=pltpu.CompilerParams(vmem_limit_bytes=32 * MIB),
        name="edge_gram",
    )(partial, before, after, ground, rows, flat, gram_basis)


def sweep(block, rank):
    lane = lanes_of(block.shape)
    for j in range(rank):
        column = jnp.broadcast_to(block[:, j : j + 1], block.shape)
        norm = jnp.sum(column * column, axis=0, keepdims=True)
        along = jnp.sum(column * block, axis=0, keepdims=True)
        part = jnp.where(lane[:1] > j, along / norm, 0.0)
        block = block - column * part
    norm = jnp.sum(block * block, axis=0, keepdims=True)
    return jnp.where(lane < rank, block / jnp.sqrt(norm), 0.0)


def frame_of(gram, rank):
    cols = gram.shape[0]
    lane, row = lanes_of(gram.shape), rows_of(gram.shape)
    frame = sweep(gram, rank)
    for _ in range(ITERS - 1):
        frame = sweep(jnp.dot(gram, frame, precision=HIGH, preferred_element_type=F32), rank)
    dots = lax.dot_general(
        frame, frame, (((0,), (0,)), ((), ())), precision=HIGH, preferred_element_type=F32
    )
    upper = jnp.where(row < lane, dots, 0.0)
    upper = upper + jnp.where(row == lane, 0.5 * (dots - 1.0), 0.0)
    upper = jnp.where(lane < rank, upper, 0.0)
    return frame - jnp.dot(frame, upper, precision=HIGH, preferred_element_type=F32)


def final_kernel(grams, flat, snap, out, lhs, held, sems):
    level = pl.program_id(0)
    rank = out.shape[0]
    wide = flat.shape[2]
    copies = [
        pltpu.make_async_copy(flat, held.at[:, :, 0:wide], sems.at[0]),
        pltpu.make_async_copy(snap, held.at[:, :, wide:], sems.at[1]),
    ]

    @pl.when(level == 0)
    def _():
        for copy in copies:
            copy.start()
        frame = frame_of(jnp.sum(grams[...], axis=0), rank)
        cols = frame.shape[0]
        high = frame.astype(BF16).astype(F32)
        low = frame - high
        spread = (rows_of((cols, cols * LON)) == lanes_of((cols, cols * LON)) // LON).astype(BF16)
        for i, part in enumerate((high, low)):
            wide_t = lax.dot_general(
                part.astype(BF16), spread, (((0,), (0,)), ((), ())), preferred_element_type=F32
            )[:rank]
            tall = jnp.broadcast_to(wide_t[:, None, :], (rank, LON, cols * LON))
            tall = tall.reshape(rank * LON, cols * LON)
            tall = jnp.where(same_lon(tall.shape), tall, 0.0)
            lhs[i * rank * LON : (i + 1) * rank * LON, :] = tall.astype(BF16)
        for copy in copies:
            copy.wait()

    for f in range(2):
        both = jnp.dot(lhs[...], held[level, f], preferred_element_type=F32)
        total = both[: rank * LON] + both[rank * LON :]
        out[:, 0, f] = total.reshape(rank, LON, total.shape[1])


def final(grams, flat, snap, rank):
    levels, fields, _, lat = flat.shape
    cols = grams.shape[-1]
    return pl.pallas_call(
        final_kernel,
        grid=(levels,),
        in_specs=[
            pl.BlockSpec(grams.shape, lambda l: (0, 0, 0)),
            pl.BlockSpec(memory_space=pl.ANY),
            pl.BlockSpec(memory_space=pl.ANY),
        ],
        out_specs=pl.BlockSpec((rank, 1, fields, LON, lat), lambda l: (0, l, 0, 0, 0)),
        out_shape=jax.ShapeDtypeStruct((rank, levels, fields, LON, lat), F32),
        scratch_shapes=[
            pltpu.VMEM((2 * rank * LON, cols * LON), BF16),
            pltpu.VMEM((levels, fields, cols * LON, lat), BF16),
            pltpu.SemaphoreType.DMA((2,)),
        ],
        compiler_params=pltpu.CompilerParams(vmem_limit_bytes=40 * MIB),
        name="frame_project",
    )(grams, flat, snap)


def on_device(winds, basis, ground):
    levels, lat = winds.shape[2], winds.shape[4]
    rank = basis.shape[0]
    tiles = lax.axis_size("tile")
    devices = tiles * lax.axis_size("band")
    up_pairs = [(i, (i + 1) % tiles) for i in range(tiles)]
    down_pairs = [(j, i) for i, j in up_pairs]

    up, down = pack(winds)
    before = lax.ppermute(up, "tile", up_pairs)
    after = lax.ppermute(down, "tile", down_pairs)

    cosine = jnp.cos((jnp.arange(lat, dtype=F32) + 0.5) * (jnp.pi / lat) - jnp.pi / 2)
    rows = jnp.stack([cosine, jnp.sqrt(cosine) / cosine / 12.0])
    rows = jnp.concatenate([rows, jnp.zeros((LON - 2, lat), F32)])
    ground = ground - lax.axis_index("band") * levels
    partial, flat, gram_basis = local(winds, basis, ground, rows)
    snap, gram = edges(partial, before, after, ground, rows, flat, gram_basis)
    copies = jnp.broadcast_to(gram[None], (devices,) + gram.shape)
    grams = lax.all_to_all(copies, ("band", "tile"), 0, 0)
    return final(grams, flat, snap, rank)


def solution(mesh):
    return jax.shard_map(
        on_device,
        mesh=mesh,
        in_specs=(
            P(None, None, "band", "tile", None),
            P(None, "band", None, "tile", None),
            P("tile", None),
        ),
        out_specs=P(None, "band", None, "tile", None),
        check_vma=False,
    )
```

```python
import jax
import jax.numpy as jnp
from jax import lax
from jax.experimental import pallas as pl
from jax.experimental.pallas import tpu as pltpu
from jax.sharding import PartitionSpec as P

ITERS = 4
HIGH = lax.Precision.HIGHEST
LON = 8
HALF = 4
TURN = 3
MIB = 1 << 20
F32 = jnp.float32
BF16 = jnp.bfloat16


def rows_of(shape):
    return lax.broadcasted_iota(jnp.int32, shape, len(shape) - 2)


def lanes_of(shape):
    return lax.broadcasted_iota(jnp.int32, shape, len(shape) - 1)


def turn_of(levels):
    return TURN if levels % TURN == 0 else 1


def whole_lanes(lat):
    return lat // 128 * 128


def ordered(row, at2, at4, at6, rest):
    return jnp.where(row < 2, at2, jnp.where(row < 4, at4, jnp.where(row < 6, at6, rest)))


def pack_kernel(winds, up, down):
    fields, snaps, turn = winds.shape[:3]
    lat = winds.shape[4]
    main = whole_lanes(lat)
    row = rows_of((LON, lat))
    odd = row % 2 == 1
    for f in range(fields):
        for g in range(snaps // 4):
            tails = ([], [])
            for i in range(turn):
                x = [winds[f, 4 * g + t, i] for t in range(4)]
                both2, both6 = pltpu.roll(x[2], 2, 0), pltpu.roll(x[3], 6, 0)
                low = ordered(row, x[0], both2, pltpu.roll(x[1], 4, 0), both6)
                low = jnp.where(odd, 8.0 * pltpu.roll(low, 1, 0), 0.0) - low
                high = ordered(row, both2, pltpu.roll(x[0], 4, 0), both6, x[1])
                high = high - jnp.where(odd, 0.0, 8.0 * pltpu.roll(high, 7, 0))
                for ref, tail, tile in ((down, tails[0], low), (up, tails[1], high)):
                    ref[f, 0, g, :, i * main : (i + 1) * main] = tile[:, :main]
                    tail.append(tile[:, main:])
            for ref, tail in ((down, tails[0]), (up, tails[1])):
                ref[f, 0, g, :, turn * main :] = jnp.concatenate(tail, axis=1)


def pack(winds):
    fields, snaps, levels, lon, lat = winds.shape
    turn = turn_of(levels)
    out = jax.ShapeDtypeStruct((fields, levels // turn, snaps // 4, lon, turn * lat), F32)
    spec = pl.BlockSpec((fields, 1) + out.shape[2:], lambda i: (0, i, 0, 0, 0))
    return pl.pallas_call(
        pack_kernel,
        grid=(levels // turn,),
        in_specs=[pl.BlockSpec((fields, snaps, turn, lon, lat), lambda i: (0, 0, i, 0, 0))],
        out_specs=[spec, spec],
        out_shape=[out, out],
        compiler_params=pltpu.CompilerParams(vmem_limit_bytes=60 * MIB),
        name="pack_halo",
    )(winds)


def lat_diff(x):
    lat = x.shape[1]
    wide = pl.cdiv(lat + 2, 128) * 128
    x = jnp.concatenate([x, jnp.zeros((LON, wide - lat), F32)], axis=1)
    near = pltpu.roll(x, wide - 1, 1) - pltpu.roll(x, 1, 1)
    far = pltpu.roll(x, wide - 2, 1) - pltpu.roll(x, 2, 1)
    return (8.0 * near - far)[:, :lat]


def lon_diff_inside(x):
    row = rows_of(x.shape)
    out = jnp.where(row < 7, 8.0 * pltpu.roll(x, 7, 0), 0.0)
    out = out - jnp.where(row > 0, 8.0 * pltpu.roll(x, 1, 0), 0.0)
    out = out - jnp.where(row < 6, pltpu.roll(x, 6, 0), 0.0)
    return out + jnp.where(row > 1, pltpu.roll(x, 2, 0), 0.0)


def parted(planes):
    inner, edge = [], []
    for one, two in zip(planes[::2], planes[1::2]):
        top = rows_of(one.shape) < HALF
        one2, one6 = pltpu.roll(one, 2, 0), pltpu.roll(one, 6, 0)
        two2, two6 = pltpu.roll(two, 2, 0), pltpu.roll(two, 6, 0)
        inner.append(jnp.where(top, one6, two2))
        edge.append(jnp.where(top, one2, two6))
    return jnp.concatenate(inner, axis=0), jnp.concatenate(edge, axis=0)


def lon_trace(prod):
    rows, cols = prod.shape
    kept = jnp.where(rows_of(prod.shape) % HALF == lanes_of(prod.shape) % HALF, prod, 0.0)
    left = (lanes_of((rows // HALF, rows)) // HALF == rows_of((rows // HALF, rows))).astype(F32)
    right = (rows_of((cols, cols // HALF)) // HALF == lanes_of((cols, cols // HALF))).astype(F32)
    kept = jnp.dot(left, kept, precision=HIGH, preferred_element_type=F32)
    return jnp.dot(kept, right, precision=HIGH, preferred_element_type=F32)


def dot_lanes(a, b):
    return lax.dot_general(a, b, (((1,), (1,)), ((), ())), preferred_element_type=F32)


def local_kernel(
    winds, basis, ground, rows, edge, basis_edge, inner, basis_inner, gram, acc_inner, acc_edge
):
    level = pl.program_id(0)
    snaps, lat = winds.shape[1], winds.shape[4]
    rank = basis.shape[0]

    @pl.when(level == 0)
    def _():
        acc_inner[...] = jnp.zeros_like(acc_inner)
        acc_edge[...] = jnp.zeros_like(acc_edge)

    cosine = jnp.broadcast_to(rows[0:1, :], (LON, lat))
    scale = jnp.where(level < ground[...], jnp.broadcast_to(rows[1:2, :], (LON, lat)), 0.0)
    fields = ([], [])
    for t in range(snaps):
        east, north = winds[0, t, 0], winds[1, t, 0]
        fields[0].append((lon_diff_inside(north) - lat_diff(east * cosine)) * scale)
        fields[1].append((lon_diff_inside(east) + lat_diff(north * cosine)) * scale)
    for f in range(2):
        inside, outside = parted(fields[f])
        edge[0, f] = outside
        inside = inside.astype(BF16)
        inner[0, f] = inside
        b_inside, b_outside = parted([basis[c, 0, f].astype(F32) for c in range(rank)])
        b_inside, b_outside = b_inside.astype(BF16), b_outside.astype(BF16)
        basis_inner[0, f] = b_inside
        basis_edge[0, f] = b_outside
        block = jnp.concatenate([b_inside, inside], axis=0)
        acc_inner[...] += dot_lanes(block, block)
        acc_edge[...] += dot_lanes(b_outside, b_outside)

    @pl.when(level == pl.num_programs(0) - 1)
    def _():
        gram[...] = lon_trace(acc_inner[...])
        gram[0:rank, 0:rank] += lon_trace(acc_edge[...])


def local(winds, basis, ground, rows):
    fields, snaps, levels, lon, lat = winds.shape
    rank = basis.shape[0]
    cols = rank + snaps

    def each(height, dtype):
        block = pl.BlockSpec((1, fields, height, lat), lambda l: (l, 0, 0, 0))
        return block, jax.ShapeDtypeStruct((levels, fields, height, lat), dtype)

    outs = [
        each(snaps * HALF, F32),
        each(rank * HALF, BF16),
        each(snaps * HALF, BF16),
        each(rank * HALF, BF16),
        (
            pl.BlockSpec((cols, cols), lambda l: (0, 0)),
            jax.ShapeDtypeStruct((cols, cols), F32),
        ),
    ]
    return pl.pallas_call(
        local_kernel,
        grid=(levels,),
        in_specs=[
            pl.BlockSpec((fields, snaps, 1, lon, lat), lambda l: (0, 0, l, 0, 0)),
            pl.BlockSpec((rank, 1, fields, lon, lat), lambda l: (0, l, 0, 0, 0)),
            pl.BlockSpec((lon, lat), lambda l: (0, 0)),
            pl.BlockSpec((LON, lat), lambda l: (0, 0)),
        ],
        out_specs=[block for block, _ in outs],
        out_shape=[shape for _, shape in outs],
        scratch_shapes=[
            pltpu.VMEM((cols * HALF, cols * HALF), F32),
            pltpu.VMEM((rank * HALF, rank * HALF), F32),
        ],
        compiler_params=pltpu.CompilerParams(vmem_limit_bytes=40 * MIB),
        cost_estimate=pl.CostEstimate(
            flops=2 * 10**9, bytes_accessed=26 * 10**6, transcendentals=0
        ),
        name="local_stencil",
    )(winds, basis, ground, rows)


def edge_kernel(before, after, part, basis_edge, ground, rows, gram, snap, copies, held, acc, sems):
    levels, fields, height, lat = part.shape
    turns, groups = before.shape[1:3]
    turn = levels // turns
    main = whole_lanes(lat)
    rank = gram.shape[0] - height // HALF
    pulls = []
    for n in range(turns):
        for i, source in enumerate((before, after)):
            pulls.append(pltpu.make_async_copy(source.at[:, n], held.at[i, n], sems.at[i, n]))
            pulls[-1].start()
    acc[...] = jnp.zeros_like(acc)
    row = rows_of((LON, lat))
    from_after = row % HALF < 2

    def tile(side, n, f, g, i):
        start = turn * main + i * (lat - main)
        return jnp.concatenate(
            [
                held[side, n, f, g, :, i * main : (i + 1) * main],
                held[side, n, f, g, :, start : start + lat - main],
            ],
            axis=1,
        )

    for n in range(turns):
        pulls[2 * n].wait()
        pulls[2 * n + 1].wait()
        for i in range(turn):
            level = n * turn + i
            scale = jnp.where(level < ground[...], jnp.broadcast_to(rows[1:2, :], (LON, lat)), 0.0)
            for f in range(fields):
                tiles = []
                for g in range(groups):
                    high, low = tile(0, n, 1 - f, g, i), tile(1, n, 1 - f, g, i)
                    tiles.append(jnp.where(from_after, low, high))
                    tiles.append(
                        jnp.where(from_after, pltpu.roll(low, 6, 0), pltpu.roll(high, 2, 0))
                    )
                tiles = [
                    part[level, f, LON * p : LON * (p + 1)] + x * scale
                    for p, x in enumerate(tiles)
                ]
                block = jnp.concatenate(tiles, axis=0).astype(BF16)
                snap[level, f] = block
                both = jnp.concatenate([basis_edge[level, f], block], axis=0)
                acc[...] += dot_lanes(block, both)

    late = lon_trace(acc[...])
    cross = jnp.concatenate([jnp.zeros((rank, rank), F32), late[:, :rank].T], axis=1)
    total = gram[...] + jnp.concatenate([cross, late], axis=0)
    cols = total.shape[0]
    lined = jnp.concatenate([total[LON * p : LON * (p + 1)] for p in range(cols // LON)], axis=1)
    copies[...] = jnp.broadcast_to(lined[None], copies.shape)


def edges(before, after, part, basis_edge, ground, rows, gram, devices):
    levels, fields, height, lat = part.shape
    cols = gram.shape[0]
    whole = pl.BlockSpec(memory_space=pltpu.VMEM)
    far = pl.BlockSpec(memory_space=pl.ANY)
    turns, groups = before.shape[1:3]
    return pl.pallas_call(
        edge_kernel,
        in_specs=[far, far, whole, whole, whole, whole, whole],
        out_specs=[whole, whole],
        out_shape=[
            jax.ShapeDtypeStruct((levels, fields, height, lat), BF16),
            jax.ShapeDtypeStruct((devices, LON, cols * cols // LON), F32),
        ],
        scratch_shapes=[
            pltpu.VMEM((2, turns, fields, groups, LON, before.shape[4]), F32),
            pltpu.VMEM((height, cols * HALF), F32),
            pltpu.SemaphoreType.DMA((2, turns)),
        ],
        compiler_params=pltpu.CompilerParams(vmem_limit_bytes=40 * MIB),
        name="edge_gram",
    )(before, after, part, basis_edge, ground, rows, gram)


def spread_lane(block, j):
    return jnp.broadcast_to(block[:, j : j + 1], block.shape)


def down_sum(x):
    return jnp.sum(x, axis=0, keepdims=True)


def sweep(block, rank):
    lane = lanes_of(block.shape)
    ahead = [spread_lane(block, j) for j in range(2)]
    for j in range(rank):
        if j + 2 < rank:
            ahead.append(spread_lane(block, j + 2))
        column = ahead.pop(0)
        inverse = 1.0 / down_sum(column * column)
        ahead = [x - column * (down_sum(column * x) * inverse) for x in ahead]
        part = jnp.where(lane[:1] > j, down_sum(column * block) * inverse, 0.0)
        block = block - column * part
    norm = down_sum(block * block)
    return jnp.where(lane < rank, block / jnp.sqrt(norm), 0.0)


def frame_of(gram, rank):
    lane, row = lanes_of(gram.shape), rows_of(gram.shape)
    frame = sweep(gram, rank)
    for _ in range(ITERS - 1):
        frame = sweep(jnp.dot(gram, frame, precision=HIGH, preferred_element_type=F32), rank)
    dots = lax.dot_general(
        frame, frame, (((0,), (0,)), ((), ())), precision=HIGH, preferred_element_type=F32
    )
    upper = jnp.where(row < lane, dots, 0.0)
    upper = upper + jnp.where(row == lane, 0.5 * (dots - 1.0), 0.0)
    upper = jnp.where(lane < rank, upper, 0.0)
    return frame - jnp.dot(frame, upper, precision=HIGH, preferred_element_type=F32)


def frame_rows(frame, rank):
    cols = frame.shape[0]
    wide = cols * LON
    near = rank * HALF

    def column(index):
        late = index >= 2 * near
        base = jnp.where(late, index - 2 * near, index)
        size = jnp.where(late, wide // 2 - near, near)
        second = base >= size
        base = jnp.where(second, base - size, base)
        lon = jnp.where(second, (index % HALF + 6) % LON, index % HALF + 2)
        return base // HALF + jnp.where(late, rank, 0), lon

    which, _ = column(lanes_of((cols, wide)))
    spread = (rows_of((cols, wide)) == which).astype(BF16)
    shape = (rank * LON, wide)
    _, lon = column(lanes_of(shape))
    kept = rows_of(shape) % LON == lon
    high = frame.astype(BF16)
    low = (frame - high.astype(F32)).astype(BF16)
    parts = []
    for part in (high, low):
        flat = lax.dot_general(
            part, spread, (((0,), (0,)), ((), ())), preferred_element_type=F32
        )[:rank]
        tall = jnp.broadcast_to(flat[:, None, :], (rank, LON, wide)).reshape(shape)
        parts.append(jnp.where(kept, tall, 0.0).astype(BF16))
    return jnp.concatenate(parts, axis=0)


def final_kernel(grams, basis_inner, basis_edge, inner, edge, out, lhs, held, sems):
    level = pl.program_id(0)
    rank = out.shape[0]
    copies, at = [], 0
    for i, source in enumerate((basis_inner, basis_edge, inner, edge)):
        height = source.shape[2]
        copies.append(pltpu.make_async_copy(source, held.at[:, :, at : at + height], sems.at[i]))
        at += height

    @pl.when(level == 0)
    def _():
        for copy in copies:
            copy.start()
        lined = jnp.sum(grams[...], axis=0)
        cols = lined.shape[1] * LON // (held.shape[2] // LON)
        gram = jnp.concatenate(
            [lined[:, cols * p : cols * (p + 1)] for p in range(cols // LON)], axis=0
        )
        lhs[...] = frame_rows(frame_of(gram, rank), rank)
        for copy in copies:
            copy.wait()

    for f in range(2):
        both = jnp.dot(lhs[...], held[level, f], preferred_element_type=F32)
        total = both[: rank * LON] + both[rank * LON :]
        out[:, 0, f] = total.reshape(rank, LON, total.shape[1])


def final(grams, basis_inner, basis_edge, inner, edge):
    levels, fields, height, lat = basis_inner.shape
    rank = height // HALF
    cols = rank + inner.shape[2] // HALF
    far = pl.BlockSpec(memory_space=pl.ANY)
    return pl.pallas_call(
        final_kernel,
        grid=(levels,),
        in_specs=[pl.BlockSpec(grams.shape, lambda l: (0, 0, 0)), far, far, far, far],
        out_specs=pl.BlockSpec((rank, 1, fields, LON, lat), lambda l: (0, l, 0, 0, 0)),
        out_shape=jax.ShapeDtypeStruct((rank, levels, fields, LON, lat), F32),
        scratch_shapes=[
            pltpu.VMEM((2 * rank * LON, cols * LON), BF16),
            pltpu.VMEM((levels, fields, cols * LON, lat), BF16),
            pltpu.SemaphoreType.DMA((4,)),
        ],
        compiler_params=pltpu.CompilerParams(vmem_limit_bytes=40 * MIB),
        name="frame_project",
    )(grams, basis_inner, basis_edge, inner, edge)


def on_device(winds, basis, ground):
    levels, lat = winds.shape[2], winds.shape[4]
    tiles = lax.axis_size("tile")
    devices = tiles * lax.axis_size("band")
    up_pairs = [(i, (i + 1) % tiles) for i in range(tiles)]
    down_pairs = [(j, i) for i, j in up_pairs]

    up, down = pack(winds)
    before = lax.ppermute(up, "tile", up_pairs)
    after = lax.ppermute(down, "tile", down_pairs)

    cosine = jnp.cos((jnp.arange(lat, dtype=F32) + 0.5) * (jnp.pi / lat) - jnp.pi / 2)
    rows = jnp.stack([cosine, jnp.sqrt(cosine) / cosine / 12.0])
    rows = jnp.concatenate([rows, jnp.zeros((LON - 2, lat), F32)])
    ground = ground - lax.axis_index("band") * levels
    ground_edge = jnp.concatenate([ground[6:], ground[:2], ground[6:], ground[:2]])
    part, basis_edge, inner, basis_inner, gram = local(winds, basis, ground, rows)
    edge, copies = edges(before, after, part, basis_edge, ground_edge, rows, gram, devices)
    grams = lax.all_to_all(copies, ("band", "tile"), 0, 0)
    return final(grams, basis_inner, basis_edge, inner, edge)


def solution(mesh):
    return jax.shard_map(
        on_device,
        mesh=mesh,
        in_specs=(
            P(None, None, "band", "tile", None),
            P(None, "band", None, "tile", None),
            P("tile", None),
        ),
        out_specs=P(None, "band", None, "tile", None),
        check_vma=False,
    )
```

```python
import functools

import jax
import jax.numpy as jnp
from jax import lax
from jax.experimental import pallas as pl
from jax.experimental.pallas import tpu as pltpu
from jax.sharding import PartitionSpec as P

ITERS = 4
HIGH = lax.Precision.HIGHEST
LON = 8
HALF = 4
TURN = 3
MIB = 1 << 20
PACK_VMEM = 56 * MIB
AHEAD = 4
F32 = jnp.float32
BF16 = jnp.bfloat16


def rows_of(shape):
    return lax.broadcasted_iota(jnp.int32, shape, len(shape) - 2)


def lanes_of(shape):
    return lax.broadcasted_iota(jnp.int32, shape, len(shape) - 1)


def turn_of(levels):
    return TURN if levels % TURN == 0 else 1


def spans_of(levels):
    if levels % 2:
        return [(0, levels)]
    return [(0, levels // 2), (levels // 2, levels // 2)]


def whole_lanes(lat):
    return lat // 128 * 128


def ordered(row, at2, at4, at6, rest):
    return jnp.where(row < 2, at2, jnp.where(row < 4, at4, jnp.where(row < 6, at6, rest)))


def pack_kernel(first, winds, *refs):
    up, down, held, sems = refs[-4:]
    fields, snaps = winds.shape[:2]
    turns, turn = held.shape[0], held.shape[3]
    lat = winds.shape[4]
    main = whole_lanes(lat)
    pulls = []
    for n in range(turns):
        levels = pl.ds(first + n * turn, turn)
        pulls.append(pltpu.make_async_copy(winds.at[:, :, levels], held.at[n], sems.at[n]))
        pulls[-1].start()
    row = rows_of((LON, lat))
    odd = row % 2 == 1
    for n in range(turns):
        pulls[n].wait()
        for f in range(fields):
            for g in range(snaps // 4):
                tails = ([], [])
                for i in range(turn):
                    x = [held[n, f, 4 * g + t, i] for t in range(4)]
                    both2, both6 = pltpu.roll(x[2], 2, 0), pltpu.roll(x[3], 6, 0)
                    low = ordered(row, x[0], both2, pltpu.roll(x[1], 4, 0), both6)
                    low = jnp.where(odd, 8.0 * pltpu.roll(low, 1, 0), 0.0) - low
                    high = ordered(row, both2, pltpu.roll(x[0], 4, 0), both6, x[1])
                    high = high - jnp.where(odd, 0.0, 8.0 * pltpu.roll(high, 7, 0))
                    for ref, tail, tile in ((down, tails[0], low), (up, tails[1], high)):
                        ref[f, n, g, :, i * main : (i + 1) * main] = tile[:, :main]
                        tail.append(tile[:, main:])
                for ref, tail in ((down, tails[0]), (up, tails[1])):
                    ref[f, n, g, :, turn * main :] = jnp.concatenate(tail, axis=1)


def pack(winds, first, count, after):
    fields, snaps, _, lon, lat = winds.shape
    turn = turn_of(count)
    turns = count // turn
    out = jax.ShapeDtypeStruct((fields, turns, snaps // 4, lon, turn * lat), F32)
    whole = pl.BlockSpec(memory_space=pltpu.VMEM)
    return pl.pallas_call(
        functools.partial(pack_kernel, first),
        in_specs=[pl.BlockSpec(memory_space=pl.ANY)] * (1 + len(after)),
        out_specs=[whole, whole],
        out_shape=[out, out],
        scratch_shapes=[
            pltpu.VMEM((turns, fields, snaps, turn, lon, lat), F32),
            pltpu.SemaphoreType.DMA((turns,)),
        ],
        compiler_params=pltpu.CompilerParams(vmem_limit_bytes=PACK_VMEM),
        name="pack_halo",
    )(winds, *after)


def lat_diff(x):
    lat = x.shape[1]
    wide = pl.cdiv(lat + 2, 128) * 128
    x = jnp.concatenate([x, jnp.zeros((LON, wide - lat), F32)], axis=1)
    near = pltpu.roll(x, wide - 1, 1) - pltpu.roll(x, 1, 1)
    far = pltpu.roll(x, wide - 2, 1) - pltpu.roll(x, 2, 1)
    return (8.0 * near - far)[:, :lat]


def lon_diff_inside(x):
    row = rows_of(x.shape)
    out = jnp.where(row < 7, 8.0 * pltpu.roll(x, 7, 0), 0.0)
    out = out - jnp.where(row > 0, 8.0 * pltpu.roll(x, 1, 0), 0.0)
    out = out - jnp.where(row < 6, pltpu.roll(x, 6, 0), 0.0)
    return out + jnp.where(row > 1, pltpu.roll(x, 2, 0), 0.0)


def parted(planes):
    inner, edge = [], []
    for one, two in zip(planes[::2], planes[1::2]):
        top = rows_of(one.shape) < HALF
        one2, one6 = pltpu.roll(one, 2, 0), pltpu.roll(one, 6, 0)
        two2, two6 = pltpu.roll(two, 2, 0), pltpu.roll(two, 6, 0)
        inner.append(jnp.where(top, one6, two2))
        edge.append(jnp.where(top, one2, two6))
    return jnp.concatenate(inner, axis=0), jnp.concatenate(edge, axis=0)


def lon_trace(prod):
    rows, cols = prod.shape
    kept = jnp.where(rows_of(prod.shape) % HALF == lanes_of(prod.shape) % HALF, prod, 0.0)
    left = (lanes_of((rows // HALF, rows)) // HALF == rows_of((rows // HALF, rows))).astype(F32)
    right = (rows_of((cols, cols // HALF)) // HALF == lanes_of((cols, cols // HALF))).astype(F32)
    kept = jnp.dot(left, kept, precision=HIGH, preferred_element_type=F32)
    return jnp.dot(kept, right, precision=HIGH, preferred_element_type=F32)


def dot_lanes(a, b):
    return lax.dot_general(a, b, (((1,), (1,)), ((), ())), preferred_element_type=F32)


def local_kernel(
    winds, basis, ground, rows, edge, basis_edge, inner, basis_inner, gram, acc_inner, acc_edge
):
    level = pl.program_id(0)
    snaps, lat = winds.shape[1], winds.shape[4]
    rank = basis.shape[0]

    @pl.when(level == 0)
    def _():
        acc_inner[...] = jnp.zeros_like(acc_inner)
        acc_edge[...] = jnp.zeros_like(acc_edge)

    cosine = jnp.broadcast_to(rows[0:1, :], (LON, lat))
    scale = jnp.where(level < ground[...], jnp.broadcast_to(rows[1:2, :], (LON, lat)), 0.0)
    fields = ([], [])
    for t in range(snaps):
        east, north = winds[0, t, 0], winds[1, t, 0]
        fields[0].append((lon_diff_inside(north) - lat_diff(east * cosine)) * scale)
        fields[1].append((lon_diff_inside(east) + lat_diff(north * cosine)) * scale)
    for f in range(2):
        inside, outside = parted(fields[f])
        edge[0, f] = outside
        inside = inside.astype(BF16)
        inner[0, f] = inside
        b_inside, b_outside = parted([basis[c, 0, f].astype(F32) for c in range(rank)])
        b_inside, b_outside = b_inside.astype(BF16), b_outside.astype(BF16)
        basis_inner[0, f] = b_inside
        basis_edge[0, f] = b_outside
        block = jnp.concatenate([b_inside, inside], axis=0)
        acc_inner[...] += dot_lanes(block, block)
        acc_edge[...] += dot_lanes(b_outside, b_outside)

    @pl.when(level == pl.num_programs(0) - 1)
    def _():
        gram[...] = lon_trace(acc_inner[...])
        gram[0:rank, 0:rank] += lon_trace(acc_edge[...])


def local(winds, basis, ground, rows):
    fields, snaps, levels, lon, lat = winds.shape
    rank = basis.shape[0]
    cols = rank + snaps

    def each(height, dtype):
        block = pl.BlockSpec((1, fields, height, lat), lambda l: (l, 0, 0, 0))
        return block, jax.ShapeDtypeStruct((levels, fields, height, lat), dtype)

    outs = [
        each(snaps * HALF, F32),
        each(rank * HALF, BF16),
        each(snaps * HALF, BF16),
        each(rank * HALF, BF16),
        (
            pl.BlockSpec((cols, cols), lambda l: (0, 0)),
            jax.ShapeDtypeStruct((cols, cols), F32),
        ),
    ]
    return pl.pallas_call(
        local_kernel,
        grid=(levels,),
        in_specs=[
            pl.BlockSpec((fields, snaps, 1, lon, lat), lambda l: (0, 0, l, 0, 0)),
            pl.BlockSpec((rank, 1, fields, lon, lat), lambda l: (0, l, 0, 0, 0)),
            pl.BlockSpec((lon, lat), lambda l: (0, 0)),
            pl.BlockSpec((LON, lat), lambda l: (0, 0)),
        ],
        out_specs=[block for block, _ in outs],
        out_shape=[shape for _, shape in outs],
        scratch_shapes=[
            pltpu.VMEM((cols * HALF, cols * HALF), F32),
            pltpu.VMEM((rank * HALF, rank * HALF), F32),
        ],
        compiler_params=pltpu.CompilerParams(vmem_limit_bytes=40 * MIB),
        cost_estimate=pl.CostEstimate(
            flops=2 * 10**9, bytes_accessed=26 * 10**6, transcendentals=0
        ),
        name="local_stencil",
    )(winds, basis, ground, rows)


def edge_kernel(
    first, last, before, after, part, basis_edge, ground, rows, gram, snap, out, held, acc, sems
):
    fields, height, lat = part.shape[1:]
    turns, groups = before.shape[1:3]
    turn = snap.shape[0] // turns
    main = whole_lanes(lat)
    rank = gram.shape[0] - height // HALF
    pulls = []
    for n in range(turns):
        for i, source in enumerate((before, after)):
            pulls.append(pltpu.make_async_copy(source.at[:, n], held.at[i, n], sems.at[i, n]))
            pulls[-1].start()
    acc[...] = jnp.zeros_like(acc)
    row = rows_of((LON, lat))
    from_after = row % HALF < 2

    def tile(side, n, f, g, i):
        start = turn * main + i * (lat - main)
        return jnp.concatenate(
            [
                held[side, n, f, g, :, i * main : (i + 1) * main],
                held[side, n, f, g, :, start : start + lat - main],
            ],
            axis=1,
        )

    for n in range(turns):
        pulls[2 * n].wait()
        pulls[2 * n + 1].wait()
        for i in range(turn):
            here = n * turn + i
            level = first + here
            scale = jnp.where(level < ground[...], jnp.broadcast_to(rows[1:2, :], (LON, lat)), 0.0)
            for f in range(fields):
                tiles = []
                for g in range(groups):
                    high, low = tile(0, n, 1 - f, g, i), tile(1, n, 1 - f, g, i)
                    tiles.append(jnp.where(from_after, low, high))
                    tiles.append(
                        jnp.where(from_after, pltpu.roll(low, 6, 0), pltpu.roll(high, 2, 0))
                    )
                tiles = [
                    part[level, f, LON * p : LON * (p + 1)] + x * scale
                    for p, x in enumerate(tiles)
                ]
                block = jnp.concatenate(tiles, axis=0).astype(BF16)
                snap[here, f] = block
                both = jnp.concatenate([basis_edge[level, f], block], axis=0)
                acc[...] += dot_lanes(block, both)

    late = lon_trace(acc[...])
    cross = jnp.concatenate([jnp.zeros((rank, rank), F32), late[:, :rank].T], axis=1)
    total = gram[...] + jnp.concatenate([cross, late], axis=0)
    if not last:
        out[...] = total
        return
    cols = total.shape[0]
    lined = jnp.concatenate([total[LON * p : LON * (p + 1)] for p in range(cols // LON)], axis=1)
    out[...] = jnp.broadcast_to(lined[None], out.shape)


def edges(before, after, part, basis_edge, ground, rows, gram, first, count, devices):
    levels, fields, height, lat = part.shape
    cols = gram.shape[0]
    last = first + count == levels
    whole = pl.BlockSpec(memory_space=pltpu.VMEM)
    far = pl.BlockSpec(memory_space=pl.ANY)
    turns, groups = before.shape[1:3]
    shape = (devices, LON, cols * cols // LON) if last else (cols, cols)
    return pl.pallas_call(
        functools.partial(edge_kernel, first, last),
        in_specs=[far, far, whole, whole, whole, whole, whole],
        out_specs=[whole, whole],
        out_shape=[
            jax.ShapeDtypeStruct((count, fields, height, lat), BF16),
            jax.ShapeDtypeStruct(shape, F32),
        ],
        scratch_shapes=[
            pltpu.VMEM((2, turns, fields, groups, LON, before.shape[4]), F32),
            pltpu.VMEM((height, cols * HALF), F32),
            pltpu.SemaphoreType.DMA((2, turns)),
        ],
        compiler_params=pltpu.CompilerParams(vmem_limit_bytes=32 * MIB),
        cost_estimate=pl.CostEstimate(
            flops=10**8, bytes_accessed=6 * 10**6, transcendentals=0
        ),
        name="edge_gram",
    )(before, after, part, basis_edge, ground, rows, gram)


def spread_lane(block, j):
    return jnp.broadcast_to(block[:, j : j + 1], block.shape)


def down_sum(x):
    return jnp.sum(x, axis=0, keepdims=True)


def sweep(block, rank):
    lane = lanes_of(block.shape)
    ahead = [spread_lane(block, j) for j in range(AHEAD)]
    for j in range(rank):
        if j + AHEAD < rank:
            ahead.append(spread_lane(block, j + AHEAD))
        column = ahead.pop(0)
        inverse = 1.0 / down_sum(column * column)
        ahead = [x - column * (down_sum(column * x) * inverse) for x in ahead]
        part = jnp.where(lane[:1] > j, down_sum(column * block) * inverse, 0.0)
        block = block - column * part
    norm = down_sum(block * block)
    return jnp.where(lane < rank, block / jnp.sqrt(norm), 0.0)


def frame_of(gram, rank):
    lane, row = lanes_of(gram.shape), rows_of(gram.shape)
    frame = sweep(gram, rank)
    for _ in range(ITERS - 1):
        frame = sweep(jnp.dot(gram, frame, precision=HIGH, preferred_element_type=F32), rank)
    dots = lax.dot_general(
        frame, frame, (((0,), (0,)), ((), ())), precision=HIGH, preferred_element_type=F32
    )
    upper = jnp.where(row < lane, dots, 0.0)
    upper = upper + jnp.where(row == lane, 0.5 * (dots - 1.0), 0.0)
    upper = jnp.where(lane < rank, upper, 0.0)
    return frame - jnp.dot(frame, upper, precision=HIGH, preferred_element_type=F32)


def frame_rows(frame, rank):
    cols = frame.shape[0]
    wide = cols * LON
    near = rank * HALF

    def column(index):
        late = index >= 2 * near
        base = jnp.where(late, index - 2 * near, index)
        size = jnp.where(late, wide // 2 - near, near)
        second = base >= size
        base = jnp.where(second, base - size, base)
        lon = jnp.where(second, (index % HALF + 6) % LON, index % HALF + 2)
        return base // HALF + jnp.where(late, rank, 0), lon

    which, _ = column(lanes_of((cols, wide)))
    spread = (rows_of((cols, wide)) == which).astype(BF16)
    shape = (rank * LON, wide)
    _, lon = column(lanes_of(shape))
    kept = rows_of(shape) % LON == lon
    high = frame.astype(BF16)
    low = (frame - high.astype(F32)).astype(BF16)
    parts = []
    for part in (high, low):
        flat = lax.dot_general(
            part, spread, (((0,), (0,)), ((), ())), preferred_element_type=F32
        )[:rank]
        tall = jnp.broadcast_to(flat[:, None, :], (rank, LON, wide)).reshape(shape)
        parts.append(jnp.where(kept, tall, 0.0).astype(BF16))
    return jnp.concatenate(parts, axis=0)


def final_kernel(grams, basis_inner, basis_edge, inner, *refs):
    edge_parts, (out, lhs, held, made, in_sems, out_sems) = refs[:-6], refs[-6:]
    rank, levels = out.shape[:2]
    pulls, at = [], 0
    for source in (basis_inner, basis_edge, inner):
        height = source.shape[2]
        pulls.append((source, held.at[:, :, at : at + height]))
        at += height
    first = 0
    for source in edge_parts:
        count, _, height = source.shape[:3]
        pulls.append((source, held.at[first : first + count, :, at : at + height]))
        first += count
    pulls = [pltpu.make_async_copy(*pull, in_sems.at[i]) for i, pull in enumerate(pulls)]
    for pull in pulls:
        pull.start()
    lined = jnp.sum(grams[...], axis=0)
    cols = held.shape[2] // LON
    gram = jnp.concatenate(
        [lined[:, cols * p : cols * (p + 1)] for p in range(cols // LON)], axis=0
    )
    lhs[...] = frame_rows(frame_of(gram, rank), rank)
    for pull in pulls:
        pull.wait()

    step = 2 if levels % 2 == 0 else 1

    def push(i):
        span = pl.ds(i * step, step)
        return pltpu.make_async_copy(made.at[:, span], out.at[:, span], out_sems.at[i])

    def project(i, carry):
        for level in range(step):
            for f in range(2):
                both = jnp.dot(
                    lhs[...], held[i * step + level, f], preferred_element_type=F32
                )
                total = both[: rank * LON] + both[rank * LON :]
                made[:, i * step + level, f] = total.reshape(rank, LON, total.shape[1])
        push(i).start()
        return carry

    def finish(i, carry):
        push(i).wait()
        return carry

    lax.fori_loop(0, levels // step, project, 0)
    lax.fori_loop(0, levels // step, finish, 0)


def final(grams, basis_inner, basis_edge, inner, edge_parts):
    levels, fields, height, lat = basis_inner.shape
    rank = height // HALF
    cols = rank + inner.shape[2] // HALF
    far = pl.BlockSpec(memory_space=pl.ANY)
    shape = (rank, levels, fields, LON, lat)
    return pl.pallas_call(
        final_kernel,
        in_specs=[pl.BlockSpec(memory_space=pltpu.VMEM)] + [far] * (3 + len(edge_parts)),
        out_specs=far,
        out_shape=jax.ShapeDtypeStruct(shape, F32),
        scratch_shapes=[
            pltpu.VMEM((2 * rank * LON, cols * LON), BF16),
            pltpu.VMEM((levels, fields, cols * LON, lat), BF16),
            pltpu.VMEM(shape, F32),
            pltpu.SemaphoreType.DMA((3 + len(edge_parts),)),
            pltpu.SemaphoreType.DMA((levels,)),
        ],
        compiler_params=pltpu.CompilerParams(vmem_limit_bytes=40 * MIB),
        name="frame_project",
    )(grams, basis_inner, basis_edge, inner, *edge_parts)


def on_device(winds, basis, ground):
    levels, lat = winds.shape[2], winds.shape[4]
    tiles = lax.axis_size("tile")
    devices = tiles * lax.axis_size("band")
    up_pairs = [(i, (i + 1) % tiles) for i in range(tiles)]
    down_pairs = [(j, i) for i, j in up_pairs]

    spans = spans_of(levels)
    halos, packed = [], ()
    for first, count in spans:
        up, down = packed = pack(winds, first, count, packed)
        halos.append((lax.ppermute(up, "tile", up_pairs), lax.ppermute(down, "tile", down_pairs)))

    cosine = jnp.cos((jnp.arange(lat, dtype=F32) + 0.5) * (jnp.pi / lat) - jnp.pi / 2)
    rows = jnp.stack([cosine, jnp.sqrt(cosine) / cosine / 12.0])
    rows = jnp.concatenate([rows, jnp.zeros((LON - 2, lat), F32)])
    ground = ground - lax.axis_index("band") * levels
    ground_edge = jnp.concatenate([ground[6:], ground[:2], ground[6:], ground[:2]])
    part, basis_edge, inner, basis_inner, gram = local(winds, basis, ground, rows)
    edge_parts = []
    for (first, count), halo in zip(spans, halos):
        edge, gram = edges(*halo, part, basis_edge, ground_edge, rows, gram, first, count, devices)
        edge_parts.append(edge)
    grams = lax.all_to_all(gram, ("band", "tile"), 0, 0)
    return final(grams, basis_inner, basis_edge, inner, edge_parts)


def solution(mesh):
    return jax.shard_map(
        on_device,
        mesh=mesh,
        in_specs=(
            P(None, None, "band", "tile", None),
            P(None, "band", None, "tile", None),
            P("tile", None),
        ),
        out_specs=P(None, "band", None, "tile", None),
        check_vma=False,
    )
```

```python
import functools

import jax
import jax.numpy as jnp
from jax import lax
from jax.experimental import pallas as pl
from jax.experimental.pallas import tpu as pltpu
from jax.sharding import PartitionSpec as P

ITERS = 4
HIGH = lax.Precision.HIGHEST
LON = 8
HALF = 4
TURN = 3
MIB = 1 << 20
LEAST_SHARE = 1e-6
AHEAD = 5
F32 = jnp.float32
BF16 = jnp.bfloat16


def rows_of(shape):
    return lax.broadcasted_iota(jnp.int32, shape, len(shape) - 2)


def lanes_of(shape):
    return lax.broadcasted_iota(jnp.int32, shape, len(shape) - 1)


def turn_of(levels):
    return TURN if levels % TURN == 0 else 1


def spans_of(levels):
    if levels % 2:
        return [(0, levels)]
    return [(0, levels // 2), (levels // 2, levels // 2)]


def whole_lanes(lat):
    return lat // 128 * 128


def ordered(row, at2, at4, at6, rest):
    return jnp.where(row < 2, at2, jnp.where(row < 4, at4, jnp.where(row < 6, at6, rest)))


def pack_kernel(first, winds, *refs):
    up, down, held, sems = refs[-4:]
    fields, snaps = winds.shape[:2]
    turns, turn = held.shape[0], held.shape[3]
    lat = winds.shape[4]
    main = whole_lanes(lat)
    pulls = []
    for n in range(turns):
        levels = pl.ds(first + n * turn, turn)
        pulls.append(pltpu.make_async_copy(winds.at[:, :, levels], held.at[n], sems.at[n]))
        pulls[-1].start()
    row = rows_of((LON, lat))
    odd = row % 2 == 1
    for n in range(turns):
        pulls[n].wait()
        for f in range(fields):
            for g in range(snaps // 4):
                tails = ([], [])
                for i in range(turn):
                    x = [held[n, f, 4 * g + t, i] for t in range(4)]
                    both2, both6 = pltpu.roll(x[2], 2, 0), pltpu.roll(x[3], 6, 0)
                    low = ordered(row, x[0], both2, pltpu.roll(x[1], 4, 0), both6)
                    low = jnp.where(odd, 8.0 * pltpu.roll(low, 1, 0), 0.0) - low
                    high = ordered(row, both2, pltpu.roll(x[0], 4, 0), both6, x[1])
                    high = high - jnp.where(odd, 0.0, 8.0 * pltpu.roll(high, 7, 0))
                    for ref, tail, tile in ((down, tails[0], low), (up, tails[1], high)):
                        ref[f, n, g, :, i * main : (i + 1) * main] = tile[:, :main]
                        tail.append(tile[:, main:])
                for ref, tail in ((down, tails[0]), (up, tails[1])):
                    ref[f, n, g, :, turn * main :] = jnp.concatenate(tail, axis=1)


def pack(winds, first, count, after):
    fields, snaps, _, lon, lat = winds.shape
    turn = turn_of(count)
    turns = count // turn
    out = jax.ShapeDtypeStruct((fields, turns, snaps // 4, lon, turn * lat), F32)
    whole = pl.BlockSpec(memory_space=pltpu.VMEM)
    return pl.pallas_call(
        functools.partial(pack_kernel, first),
        in_specs=[pl.BlockSpec(memory_space=pltpu.HBM)]
        + [pl.BlockSpec(memory_space=pl.ANY)] * len(after),
        out_specs=[whole, whole],
        out_shape=[out, out],
        scratch_shapes=[
            pltpu.VMEM((turns, fields, snaps, turn, lon, lat), F32),
            pltpu.SemaphoreType.DMA((turns,)),
        ],
        compiler_params=pltpu.CompilerParams(vmem_limit_bytes=52 * MIB),
        name="pack_halo",
    )(winds, *after)


def lat_diff(x):
    lat = x.shape[1]
    wide = pl.cdiv(lat + 2, 128) * 128
    x = jnp.concatenate([x, jnp.zeros((LON, wide - lat), F32)], axis=1)
    near = pltpu.roll(x, wide - 1, 1) - pltpu.roll(x, 1, 1)
    far = pltpu.roll(x, wide - 2, 1) - pltpu.roll(x, 2, 1)
    return (8.0 * near - far)[:, :lat]


def lon_diff_inside(x):
    row = rows_of(x.shape)
    out = jnp.where(row < 7, 8.0 * pltpu.roll(x, 7, 0), 0.0)
    out = out - jnp.where(row > 0, 8.0 * pltpu.roll(x, 1, 0), 0.0)
    out = out - jnp.where(row < 6, pltpu.roll(x, 6, 0), 0.0)
    return out + jnp.where(row > 1, pltpu.roll(x, 2, 0), 0.0)


def parted(planes):
    inner, edge = [], []
    for one, two in zip(planes[::2], planes[1::2]):
        top = rows_of(one.shape) < HALF
        one2, one6 = pltpu.roll(one, 2, 0), pltpu.roll(one, 6, 0)
        two2, two6 = pltpu.roll(two, 2, 0), pltpu.roll(two, 6, 0)
        inner.append(jnp.where(top, one6, two2))
        edge.append(jnp.where(top, one2, two6))
    return jnp.concatenate(inner, axis=0), jnp.concatenate(edge, axis=0)


def lon_trace(prod):
    rows, cols = prod.shape
    kept = jnp.where(rows_of(prod.shape) % HALF == lanes_of(prod.shape) % HALF, prod, 0.0)
    left = (lanes_of((rows // HALF, rows)) // HALF == rows_of((rows // HALF, rows))).astype(F32)
    right = (rows_of((cols, cols // HALF)) // HALF == lanes_of((cols, cols // HALF))).astype(F32)
    kept = jnp.dot(left, kept, precision=HIGH, preferred_element_type=F32)
    return jnp.dot(kept, right, precision=HIGH, preferred_element_type=F32)


def dot_lanes(a, b):
    return lax.dot_general(a, b, (((1,), (1,)), ((), ())), preferred_element_type=F32)


def local_kernel(
    winds, basis, ground, rows, edge, basis_edge, inner, basis_inner, gram, acc_inner, acc_edge
):
    level = pl.program_id(0)
    snaps, lat = winds.shape[1], winds.shape[4]
    rank = basis.shape[0]

    @pl.when(level == 0)
    def _():
        acc_inner[...] = jnp.zeros_like(acc_inner)
        acc_edge[...] = jnp.zeros_like(acc_edge)

    cosine = jnp.broadcast_to(rows[0:1, :], (LON, lat))
    scale = jnp.where(level < ground[...], jnp.broadcast_to(rows[1:2, :], (LON, lat)), 0.0)
    fields = ([], [])
    for t in range(snaps):
        east, north = winds[0, t, 0], winds[1, t, 0]
        fields[0].append((lon_diff_inside(north) - lat_diff(east * cosine)) * scale)
        fields[1].append((lon_diff_inside(east) + lat_diff(north * cosine)) * scale)
    for f in range(2):
        inside, outside = parted(fields[f])
        edge[0, f] = outside
        inside = inside.astype(BF16)
        inner[0, f] = inside
        b_inside, b_outside = parted([basis[c, 0, f].astype(F32) for c in range(rank)])
        b_inside, b_outside = b_inside.astype(BF16), b_outside.astype(BF16)
        basis_inner[0, f] = b_inside
        basis_edge[0, f] = b_outside
        block = jnp.concatenate([b_inside, inside], axis=0)
        acc_inner[...] += dot_lanes(block, block)
        acc_edge[...] += dot_lanes(b_outside, b_outside)

    @pl.when(level == pl.num_programs(0) - 1)
    def _():
        gram[...] = lon_trace(acc_inner[...])
        gram[0:rank, 0:rank] += lon_trace(acc_edge[...])


def local(winds, basis, ground, rows):
    fields, snaps, levels, lon, lat = winds.shape
    rank = basis.shape[0]
    cols = rank + snaps

    def each(height, dtype):
        block = pl.BlockSpec((1, fields, height, lat), lambda l: (l, 0, 0, 0))
        return block, jax.ShapeDtypeStruct((levels, fields, height, lat), dtype)

    outs = [
        each(snaps * HALF, F32),
        each(rank * HALF, BF16),
        each(snaps * HALF, BF16),
        each(rank * HALF, BF16),
        (
            pl.BlockSpec((cols, cols), lambda l: (0, 0)),
            jax.ShapeDtypeStruct((cols, cols), F32),
        ),
    ]
    return pl.pallas_call(
        local_kernel,
        grid=(levels,),
        in_specs=[
            pl.BlockSpec((fields, snaps, 1, lon, lat), lambda l: (0, 0, l, 0, 0)),
            pl.BlockSpec((rank, 1, fields, lon, lat), lambda l: (0, l, 0, 0, 0)),
            pl.BlockSpec((lon, lat), lambda l: (0, 0)),
            pl.BlockSpec((LON, lat), lambda l: (0, 0)),
        ],
        out_specs=[block for block, _ in outs],
        out_shape=[shape for _, shape in outs],
        scratch_shapes=[
            pltpu.VMEM((cols * HALF, cols * HALF), F32),
            pltpu.VMEM((rank * HALF, rank * HALF), F32),
        ],
        compiler_params=pltpu.CompilerParams(vmem_limit_bytes=40 * MIB),
        cost_estimate=pl.CostEstimate(
            flops=2 * 10**9, bytes_accessed=26 * 10**6, transcendentals=0
        ),
        name="local_stencil",
    )(winds, basis, ground, rows)


def edge_kernel(
    first, last, before, after, part, basis_edge, ground, rows, gram, snap, out, acc
):
    fields, height, lat = part.shape[1:]
    turns, groups = before.shape[1:3]
    turn = snap.shape[0] // turns
    main = whole_lanes(lat)
    rank = gram.shape[0] - height // HALF
    acc[...] = jnp.zeros_like(acc)
    row = rows_of((LON, lat))
    from_after = row % HALF < 2

    def tile(halo, n, f, g, i):
        start = turn * main + i * (lat - main)
        return jnp.concatenate(
            [
                halo[f, n, g, :, i * main : (i + 1) * main],
                halo[f, n, g, :, start : start + lat - main],
            ],
            axis=1,
        )

    for n in range(turns):
        for i in range(turn):
            here = n * turn + i
            level = first + here
            scale = jnp.where(level < ground[...], jnp.broadcast_to(rows[1:2, :], (LON, lat)), 0.0)
            for f in range(fields):
                tiles = []
                for g in range(groups):
                    high, low = tile(before, n, 1 - f, g, i), tile(after, n, 1 - f, g, i)
                    tiles.append(jnp.where(from_after, low, high))
                    tiles.append(
                        jnp.where(from_after, pltpu.roll(low, 6, 0), pltpu.roll(high, 2, 0))
                    )
                tiles = [
                    part[level, f, LON * p : LON * (p + 1)] + x * scale
                    for p, x in enumerate(tiles)
                ]
                block = jnp.concatenate(tiles, axis=0).astype(BF16)
                snap[here, f] = block
                both = jnp.concatenate([basis_edge[level, f], block], axis=0)
                acc[...] += dot_lanes(block, both)

    late = lon_trace(acc[...])
    cross = jnp.concatenate([jnp.zeros((rank, rank), F32), late[:, :rank].T], axis=1)
    total = gram[...] + jnp.concatenate([cross, late], axis=0)
    if not last:
        out[...] = total
        return
    cols = total.shape[0]
    lined = jnp.concatenate([total[LON * p : LON * (p + 1)] for p in range(cols // LON)], axis=1)
    out[...] = jnp.broadcast_to(lined[None], out.shape)


def edges(before, after, part, basis_edge, ground, rows, gram, first, count, devices):
    levels, fields, height, lat = part.shape
    cols = gram.shape[0]
    last = first + count == levels
    whole = pl.BlockSpec(memory_space=pltpu.VMEM)
    shape = (devices, LON, cols * cols // LON) if last else (cols, cols)
    return pl.pallas_call(
        functools.partial(edge_kernel, first, last),
        in_specs=[whole] * 7,
        out_specs=[whole, whole],
        out_shape=[
            jax.ShapeDtypeStruct((count, fields, height, lat), BF16),
            jax.ShapeDtypeStruct(shape, F32),
        ],
        scratch_shapes=[pltpu.VMEM((height, cols * HALF), F32)],
        compiler_params=pltpu.CompilerParams(vmem_limit_bytes=32 * MIB),
        cost_estimate=pl.CostEstimate(
            flops=10**8, bytes_accessed=6 * 10**6, transcendentals=0
        ),
        name="edge_gram",
    )(before, after, part, basis_edge, ground, rows, gram)


def spread_lane(block, j):
    return jnp.broadcast_to(block[:, j : j + 1], block.shape)


def down_sum(x):
    return jnp.sum(x, axis=0, keepdims=True)


def sweep(block, rank):
    lane = lanes_of(block.shape)
    whole = down_sum(block * block)
    ahead = [spread_lane(block, j) for j in range(AHEAD)]
    for j in range(rank):
        if j + AHEAD < rank:
            ahead.append(spread_lane(block, j + AHEAD))
        column = ahead.pop(0)
        inverse = 1.0 / down_sum(column * column)
        ahead = [x - column * (down_sum(column * x) * inverse) for x in ahead]
        part = jnp.where(lane[:1] > j, down_sum(column * block) * inverse, 0.0)
        block = block - column * part
    norm = down_sum(block * block)
    share = jnp.where(lane[:1] < rank, norm / whole, 1.0)
    return jnp.where(lane < rank, block / jnp.sqrt(norm), 0.0), share


def times(a, b):
    return jnp.dot(a, b, precision=HIGH, preferred_element_type=F32)


def unit(block, rank):
    scaled = block * lax.rsqrt(down_sum(block * block))
    return jnp.where(lanes_of(block.shape) < rank, scaled, 0.0)


def once_more(frame, rank):
    lane, row = lanes_of(frame.shape), rows_of(frame.shape)
    dots = lax.dot_general(
        frame, frame, (((0,), (0,)), ((), ())), precision=HIGH, preferred_element_type=F32
    )
    upper = jnp.where(row < lane, dots, 0.0)
    upper = upper + jnp.where(row == lane, 0.5 * (dots - 1.0), 0.0)
    return frame - times(frame, jnp.where(lane < rank, upper, 0.0))


def put_frame(gram, rank, frame_ref):
    frame, lost = None, jnp.zeros((1, gram.shape[1]), F32)
    for _ in range(ITERS // 2):
        frame = gram if frame is None else times(gram, frame)
        frame, share = sweep(times(gram, unit(frame, rank)), rank)
        lost = lost + jnp.where(share >= LEAST_SHARE, 0.0, 1.0)
    frame_ref[...] = once_more(frame, rank)

    @pl.when(jnp.sum(lost) > 0.5)
    def _():
        frame, _ = sweep(gram, rank)
        for _ in range(ITERS - 1):
            frame, _ = sweep(times(gram, frame), rank)
        frame_ref[...] = once_more(frame, rank)


def frame_rows(frame, rank):
    cols = frame.shape[0]
    wide = cols * LON
    near = rank * HALF

    def column(index):
        late = index >= 2 * near
        base = jnp.where(late, index - 2 * near, index)
        size = jnp.where(late, wide // 2 - near, near)
        second = base >= size
        base = jnp.where(second, base - size, base)
        lon = jnp.where(second, (index % HALF + 6) % LON, index % HALF + 2)
        return base // HALF + jnp.where(late, rank, 0), lon

    which, _ = column(lanes_of((cols, wide)))
    spread = (rows_of((cols, wide)) == which).astype(BF16)
    shape = (rank * LON, wide)
    _, lon = column(lanes_of(shape))
    kept = rows_of(shape) % LON == lon
    high = frame.astype(BF16)
    low = (frame - high.astype(F32)).astype(BF16)
    parts = []
    for part in (high, low):
        flat = lax.dot_general(
            part, spread, (((0,), (0,)), ((), ())), preferred_element_type=F32
        )[:rank]
        tall = jnp.broadcast_to(flat[:, None, :], (rank, LON, wide)).reshape(shape)
        parts.append(jnp.where(kept, tall, 0.0).astype(BF16))
    return jnp.concatenate(parts, axis=0)


def final_kernel(grams, basis_inner, basis_edge, inner, *refs):
    edge_parts, (out, frame, lhs, made, sems) = refs[:-5], refs[-5:]
    rank, levels = out.shape[:2]
    lined = jnp.sum(grams[...], axis=0)
    cols = frame.shape[0]
    gram = jnp.concatenate(
        [lined[:, cols * p : cols * (p + 1)] for p in range(cols // LON)], axis=0
    )
    put_frame(gram, rank, frame)
    lhs[...] = frame_rows(frame[...], rank)

    def push(level, count, sem):
        span = pl.ds(level, count)
        return pltpu.make_async_copy(made.at[:, span], out.at[:, span], sems.at[sem])

    def project(edge, base, level):
        for f in range(2):
            rows = [basis_inner[level, f], basis_edge[level, f], inner[level, f], edge[level - base, f]]
            both = jnp.dot(
                lhs[...], jnp.concatenate(rows, axis=0), preferred_element_type=F32
            )
            total = both[: rank * LON] + both[rank * LON :]
            made[:, level, f] = total.reshape(rank, LON, total.shape[1])

    spans, base = [], 0
    for edge in edge_parts:
        count = edge.shape[0]
        alone = 2 - count % 2 if base == 0 else count % 2
        for level in range(base, base + alone):
            project(edge, base, level)
            push(level, 1, level).start()
            spans.append((level, 1))

        def pair(i, carry, edge=edge, base=base, start=base + alone):
            level = start + 2 * i
            project(edge, base, level)
            project(edge, base, level + 1)
            push(level, 2, level).start()
            return carry

        lax.fori_loop(0, (count - alone) // 2, pair, 0)
        spans += [(level, 2) for level in range(base + alone, base + count, 2)]
        base += count
    for level, count in spans:
        push(level, count, level).wait()


def final(grams, basis_inner, basis_edge, inner, edge_parts):
    levels, fields, height, lat = basis_inner.shape
    rank = height // HALF
    cols = rank + inner.shape[2] // HALF
    shape = (rank, levels, fields, LON, lat)
    return pl.pallas_call(
        final_kernel,
        in_specs=[pl.BlockSpec(memory_space=pltpu.VMEM)] * (4 + len(edge_parts)),
        out_specs=pl.BlockSpec(memory_space=pltpu.HBM),
        out_shape=jax.ShapeDtypeStruct(shape, F32),
        scratch_shapes=[
            pltpu.VMEM((cols, cols), F32),
            pltpu.VMEM((2 * rank * LON, cols * LON), BF16),
            pltpu.VMEM(shape, F32),
            pltpu.SemaphoreType.DMA((levels,)),
        ],
        compiler_params=pltpu.CompilerParams(vmem_limit_bytes=32 * MIB),
        name="frame_project",
    )(grams, basis_inner, basis_edge, inner, *edge_parts)


def on_device(winds, basis, ground):
    levels, lat = winds.shape[2], winds.shape[4]
    tiles = lax.axis_size("tile")
    devices = tiles * lax.axis_size("band")
    up_pairs = [(i, (i + 1) % tiles) for i in range(tiles)]
    down_pairs = [(j, i) for i, j in up_pairs]

    spans = spans_of(levels)
    halos, packed = [], ()
    for first, count in spans:
        up, down = packed = pack(winds, first, count, packed)
        halos.append((lax.ppermute(up, "tile", up_pairs), lax.ppermute(down, "tile", down_pairs)))

    cosine = jnp.cos((jnp.arange(lat, dtype=F32) + 0.5) * (jnp.pi / lat) - jnp.pi / 2)
    rows = jnp.stack([cosine, jnp.sqrt(cosine) / cosine / 12.0])
    rows = jnp.concatenate([rows, jnp.zeros((LON - 2, lat), F32)])
    ground = ground - lax.axis_index("band") * levels
    ground_edge = jnp.concatenate([ground[6:], ground[:2], ground[6:], ground[:2]])
    part, basis_edge, inner, basis_inner, gram = local(winds, basis, ground, rows)
    edge_parts = []
    for (first, count), halo in zip(spans, halos):
        edge, gram = edges(*halo, part, basis_edge, ground_edge, rows, gram, first, count, devices)
        edge_parts.append(edge)
    grams = lax.all_to_all(gram, ("band", "tile"), 0, 0)
    return final(grams, basis_inner, basis_edge, inner, edge_parts)


def solution(mesh):
    return jax.shard_map(
        on_device,
        mesh=mesh,
        in_specs=(
            P(None, None, "band", "tile", None),
            P(None, "band", None, "tile", None),
            P("tile", None),
        ),
        out_specs=P(None, "band", None, "tile", None),
        check_vma=False,
    )
```

```python
import functools

import jax
import jax.numpy as jnp
from jax import lax
from jax.experimental import pallas as pl
from jax.experimental.pallas import tpu as pltpu
from jax.sharding import PartitionSpec as P

ITERS = 4
HIGH = lax.Precision.HIGHEST
LON = 8
HALF = 4
TURN = 3
MIB = 1 << 20
LEAST_SHARE = 1e-6
AHEAD = 5
F32 = jnp.float32
BF16 = jnp.bfloat16


def rows_of(shape):
    return lax.broadcasted_iota(jnp.int32, shape, len(shape) - 2)


def lanes_of(shape):
    return lax.broadcasted_iota(jnp.int32, shape, len(shape) - 1)


def turn_of(levels):
    return TURN if levels % TURN == 0 else 1


def spans_of(levels):
    if levels % 2:
        return [(0, levels)]
    return [(0, levels // 2), (levels // 2, levels // 2)]


def whole_lanes(lat):
    return lat // 128 * 128


def ordered(row, at2, at4, at6, rest):
    return jnp.where(row < 2, at2, jnp.where(row < 4, at4, jnp.where(row < 6, at6, rest)))


def pack_kernel(first, winds, *refs):
    up, down, held, sems = refs[-4:]
    fields, snaps = winds.shape[:2]
    turns, turn = held.shape[0], held.shape[3]
    lat = winds.shape[4]
    main = whole_lanes(lat)
    pulls = []
    for n in range(turns):
        levels = pl.ds(first + n * turn, turn)
        pulls.append(pltpu.make_async_copy(winds.at[:, :, levels], held.at[n], sems.at[n]))
        pulls[-1].start()
    row = rows_of((LON, lat))
    odd = row % 2 == 1
    for n in range(turns):
        pulls[n].wait()
        for f in range(fields):
            for g in range(snaps // 4):
                tails = ([], [])
                for i in range(turn):
                    x = [held[n, f, 4 * g + t, i] for t in range(4)]
                    both2, both6 = pltpu.roll(x[2], 2, 0), pltpu.roll(x[3], 6, 0)
                    low = ordered(row, x[0], both2, pltpu.roll(x[1], 4, 0), both6)
                    low = jnp.where(odd, 8.0 * pltpu.roll(low, 1, 0), 0.0) - low
                    high = ordered(row, both2, pltpu.roll(x[0], 4, 0), both6, x[1])
                    high = high - jnp.where(odd, 0.0, 8.0 * pltpu.roll(high, 7, 0))
                    for ref, tail, tile in ((down, tails[0], low), (up, tails[1], high)):
                        ref[f, n, g, :, i * main : (i + 1) * main] = tile[:, :main]
                        tail.append(tile[:, main:])
                for ref, tail in ((down, tails[0]), (up, tails[1])):
                    ref[f, n, g, :, turn * main :] = jnp.concatenate(tail, axis=1)


def pack(winds, first, count, after):
    fields, snaps, _, lon, lat = winds.shape
    turn = turn_of(count)
    turns = count // turn
    out = jax.ShapeDtypeStruct((fields, turns, snaps // 4, lon, turn * lat), F32)
    whole = pl.BlockSpec(memory_space=pltpu.VMEM)
    return pl.pallas_call(
        functools.partial(pack_kernel, first),
        in_specs=[pl.BlockSpec(memory_space=pltpu.HBM)]
        + [pl.BlockSpec(memory_space=pl.ANY)] * len(after),
        out_specs=[whole, whole],
        out_shape=[out, out],
        scratch_shapes=[
            pltpu.VMEM((turns, fields, snaps, turn, lon, lat), F32),
            pltpu.SemaphoreType.DMA((turns,)),
        ],
        compiler_params=pltpu.CompilerParams(vmem_limit_bytes=52 * MIB),
        name="pack_halo",
    )(winds, *after)


def lat_diff(x):
    lat = x.shape[1]
    wide = pl.cdiv(lat + 2, 128) * 128
    x = jnp.concatenate([x, jnp.zeros((LON, wide - lat), F32)], axis=1)
    near = pltpu.roll(x, wide - 1, 1) - pltpu.roll(x, 1, 1)
    far = pltpu.roll(x, wide - 2, 1) - pltpu.roll(x, 2, 1)
    return (8.0 * near - far)[:, :lat]


def lon_diff_inside(x):
    row = rows_of(x.shape)
    out = jnp.where(row < 7, 8.0 * pltpu.roll(x, 7, 0), 0.0)
    out = out - jnp.where(row > 0, 8.0 * pltpu.roll(x, 1, 0), 0.0)
    out = out - jnp.where(row < 6, pltpu.roll(x, 6, 0), 0.0)
    return out + jnp.where(row > 1, pltpu.roll(x, 2, 0), 0.0)


def parted(planes):
    inner, edge = [], []
    for one, two in zip(planes[::2], planes[1::2]):
        top = rows_of(one.shape) < HALF
        one2, one6 = pltpu.roll(one, 2, 0), pltpu.roll(one, 6, 0)
        two2, two6 = pltpu.roll(two, 2, 0), pltpu.roll(two, 6, 0)
        inner.append(jnp.where(top, one6, two2))
        edge.append(jnp.where(top, one2, two6))
    return jnp.concatenate(inner, axis=0), jnp.concatenate(edge, axis=0)


def lon_trace(prod):
    rows, cols = prod.shape
    kept = jnp.where(rows_of(prod.shape) % HALF == lanes_of(prod.shape) % HALF, prod, 0.0)
    left = (lanes_of((rows // HALF, rows)) // HALF == rows_of((rows // HALF, rows))).astype(F32)
    right = (rows_of((cols, cols // HALF)) // HALF == lanes_of((cols, cols // HALF))).astype(F32)
    kept = jnp.dot(left, kept, precision=HIGH, preferred_element_type=F32)
    return jnp.dot(kept, right, precision=HIGH, preferred_element_type=F32)


def dot_lanes(a, b):
    return lax.dot_general(a, b, (((1,), (1,)), ((), ())), preferred_element_type=F32)


def local_kernel(
    winds, basis, ground, rows, edge, basis_edge, inner, basis_inner, gram, acc_inner, acc_edge
):
    level = pl.program_id(0)
    snaps, lat = winds.shape[1], winds.shape[4]
    rank = basis.shape[0]

    @pl.when(level == 0)
    def _():
        acc_inner[...] = jnp.zeros_like(acc_inner)
        acc_edge[...] = jnp.zeros_like(acc_edge)

    cosine = jnp.broadcast_to(rows[0:1, :], (LON, lat))
    scale = jnp.where(level < ground[...], jnp.broadcast_to(rows[1:2, :], (LON, lat)), 0.0)
    fields = ([], [])
    for t in range(snaps):
        east, north = winds[0, t, 0], winds[1, t, 0]
        fields[0].append((lon_diff_inside(north) - lat_diff(east * cosine)) * scale)
        fields[1].append((lon_diff_inside(east) + lat_diff(north * cosine)) * scale)
    for f in range(2):
        inside, outside = parted(fields[f])
        edge[0, f] = outside
        inside = inside.astype(BF16)
        inner[0, f] = inside
        b_inside, b_outside = parted([basis[c, 0, f].astype(F32) for c in range(rank)])
        b_inside, b_outside = b_inside.astype(BF16), b_outside.astype(BF16)
        basis_inner[0, f] = b_inside
        basis_edge[0, f] = b_outside
        block = jnp.concatenate([b_inside, inside], axis=0)
        acc_inner[...] += dot_lanes(block, block)
        acc_edge[...] += dot_lanes(b_outside, b_outside)

    @pl.when(level == pl.num_programs(0) - 1)
    def _():
        gram[...] = lon_trace(acc_inner[...])
        gram[0:rank, 0:rank] += lon_trace(acc_edge[...])


def local(winds, basis, ground, rows):
    fields, snaps, levels, lon, lat = winds.shape
    rank = basis.shape[0]
    cols = rank + snaps

    def each(height, dtype):
        block = pl.BlockSpec((1, fields, height, lat), lambda l: (l, 0, 0, 0))
        return block, jax.ShapeDtypeStruct((levels, fields, height, lat), dtype)

    outs = [
        each(snaps * HALF, F32),
        each(rank * HALF, BF16),
        each(snaps * HALF, BF16),
        each(rank * HALF, BF16),
        (
            pl.BlockSpec((cols, cols), lambda l: (0, 0)),
            jax.ShapeDtypeStruct((cols, cols), F32),
        ),
    ]
    return pl.pallas_call(
        local_kernel,
        grid=(levels,),
        in_specs=[
            pl.BlockSpec((fields, snaps, 1, lon, lat), lambda l: (0, 0, l, 0, 0)),
            pl.BlockSpec((rank, 1, fields, lon, lat), lambda l: (0, l, 0, 0, 0)),
            pl.BlockSpec((lon, lat), lambda l: (0, 0)),
            pl.BlockSpec((LON, lat), lambda l: (0, 0)),
        ],
        out_specs=[block for block, _ in outs],
        out_shape=[shape for _, shape in outs],
        scratch_shapes=[
            pltpu.VMEM((cols * HALF, cols * HALF), F32),
            pltpu.VMEM((rank * HALF, rank * HALF), F32),
        ],
        compiler_params=pltpu.CompilerParams(vmem_limit_bytes=40 * MIB),
        cost_estimate=pl.CostEstimate(
            flops=2 * 10**9, bytes_accessed=26 * 10**6, transcendentals=0
        ),
        name="local_stencil",
    )(winds, basis, ground, rows)


def edge_kernel(
    first, last, before, after, part, basis_edge, ground, rows, gram, snap, out, acc
):
    fields, height, lat = part.shape[1:]
    turns, groups = before.shape[1:3]
    turn = snap.shape[0] // turns
    main = whole_lanes(lat)
    rank = gram.shape[0] - height // HALF
    acc[...] = jnp.zeros_like(acc)
    row = rows_of((LON, lat))
    from_after = row % HALF < 2

    def tile(halo, n, f, g, i):
        start = turn * main + i * (lat - main)
        return jnp.concatenate(
            [
                halo[f, n, g, :, i * main : (i + 1) * main],
                halo[f, n, g, :, start : start + lat - main],
            ],
            axis=1,
        )

    for n in range(turns):
        for i in range(turn):
            here = n * turn + i
            level = first + here
            scale = jnp.where(level < ground[...], jnp.broadcast_to(rows[1:2, :], (LON, lat)), 0.0)
            for f in range(fields):
                tiles = []
                for g in range(groups):
                    high, low = tile(before, n, 1 - f, g, i), tile(after, n, 1 - f, g, i)
                    tiles.append(jnp.where(from_after, low, high))
                    tiles.append(
                        jnp.where(from_after, pltpu.roll(low, 6, 0), pltpu.roll(high, 2, 0))
                    )
                tiles = [
                    part[level, f, LON * p : LON * (p + 1)] + x * scale
                    for p, x in enumerate(tiles)
                ]
                block = jnp.concatenate(tiles, axis=0).astype(BF16)
                snap[here, f] = block
                both = jnp.concatenate([basis_edge[level, f], block], axis=0)
                acc[...] += dot_lanes(block, both)

    late = lon_trace(acc[...])
    cross = jnp.concatenate([jnp.zeros((rank, rank), F32), late[:, :rank].T], axis=1)
    total = gram[...] + jnp.concatenate([cross, late], axis=0)
    if not last:
        out[...] = total
        return
    cols = total.shape[0]
    lined = jnp.concatenate([total[LON * p : LON * (p + 1)] for p in range(cols // LON)], axis=1)
    out[...] = jnp.broadcast_to(lined[None], out.shape)


def edges(before, after, part, basis_edge, ground, rows, gram, first, count, devices):
    levels, fields, height, lat = part.shape
    cols = gram.shape[0]
    last = first + count == levels
    whole = pl.BlockSpec(memory_space=pltpu.VMEM)
    shape = (devices, LON, cols * cols // LON) if last else (cols, cols)
    return pl.pallas_call(
        functools.partial(edge_kernel, first, last),
        in_specs=[whole] * 7,
        out_specs=[whole, whole],
        out_shape=[
            jax.ShapeDtypeStruct((count, fields, height, lat), BF16),
            jax.ShapeDtypeStruct(shape, F32),
        ],
        scratch_shapes=[pltpu.VMEM((height, cols * HALF), F32)],
        compiler_params=pltpu.CompilerParams(vmem_limit_bytes=32 * MIB),
        cost_estimate=pl.CostEstimate(
            flops=10**8, bytes_accessed=6 * 10**6, transcendentals=0
        ),
        name="edge_gram",
    )(before, after, part, basis_edge, ground, rows, gram)


def spread_lane(block, j):
    return jnp.broadcast_to(block[:, j : j + 1], block.shape)


def down_sum(x):
    return jnp.sum(x, axis=0, keepdims=True)


def sweep(block, rank):
    lane = lanes_of(block.shape)
    whole = down_sum(block * block)
    ahead = [spread_lane(block, j) for j in range(AHEAD)]
    for j in range(rank):
        if j + AHEAD < rank:
            ahead.append(spread_lane(block, j + AHEAD))
        column = ahead.pop(0)
        inverse = 1.0 / down_sum(column * column)
        ahead = [x - column * (down_sum(column * x) * inverse) for x in ahead]
        part = jnp.where(lane[:1] > j, down_sum(column * block) * inverse, 0.0)
        block = block - column * part
    norm = down_sum(block * block)
    share = jnp.where(lane[:1] < rank, norm / whole, 1.0)
    return jnp.where(lane < rank, block / jnp.sqrt(norm), 0.0), share


def times(a, b):
    return jnp.dot(a, b, precision=HIGH, preferred_element_type=F32)


def unit(block, rank):
    scaled = block * lax.rsqrt(down_sum(block * block))
    return jnp.where(lanes_of(block.shape) < rank, scaled, 0.0)


def once_more(frame, rank):
    lane, row = lanes_of(frame.shape), rows_of(frame.shape)
    dots = lax.dot_general(
        frame, frame, (((0,), (0,)), ((), ())), precision=HIGH, preferred_element_type=F32
    )
    upper = jnp.where(row < lane, dots, 0.0)
    upper = upper + jnp.where(row == lane, 0.5 * (dots - 1.0), 0.0)
    return frame - times(frame, jnp.where(lane < rank, upper, 0.0))


def put_frame(gram, rank, frame_ref):
    frame, lost = None, jnp.zeros((1, gram.shape[1]), F32)
    for _ in range(ITERS // 2):
        frame = gram if frame is None else times(gram, frame)
        frame, share = sweep(times(gram, unit(frame, rank)), rank)
        lost = lost + jnp.where(share >= LEAST_SHARE, 0.0, 1.0)
    frame_ref[...] = once_more(frame, rank)

    @pl.when(jnp.sum(lost) > 0.5)
    def _():
        frame, _ = sweep(gram, rank)
        for _ in range(ITERS - 1):
            frame, _ = sweep(times(gram, frame), rank)
        frame_ref[...] = once_more(frame, rank)


def frame_rows(frame, rank):
    cols = frame.shape[0]
    wide = cols * LON
    near = rank * HALF

    def column(index):
        late = index >= 2 * near
        base = jnp.where(late, index - 2 * near, index)
        size = jnp.where(late, wide // 2 - near, near)
        second = base >= size
        base = jnp.where(second, base - size, base)
        lon = jnp.where(second, (index % HALF + 6) % LON, index % HALF + 2)
        return base // HALF + jnp.where(late, rank, 0), lon

    which, _ = column(lanes_of((cols, wide)))
    spread = (rows_of((cols, wide)) == which).astype(BF16)
    shape = (rank * LON, wide)
    _, lon = column(lanes_of(shape))
    kept = rows_of(shape) % LON == lon
    high = frame.astype(BF16)
    low = (frame - high.astype(F32)).astype(BF16)
    parts = []
    for part in (high, low):
        flat = lax.dot_general(
            part, spread, (((0,), (0,)), ((), ())), preferred_element_type=F32
        )[:rank]
        tall = jnp.broadcast_to(flat[:, None, :], (rank, LON, wide)).reshape(shape)
        parts.append(jnp.where(kept, tall, 0.0).astype(BF16))
    return jnp.concatenate(parts, axis=0)


def final_kernel(grams, basis_inner, basis_edge, inner, *refs):
    edge_parts, (out, frame, lhs, made, sems) = refs[:-5], refs[-5:]
    rank, levels = out.shape[:2]
    lined = jnp.sum(grams[...], axis=0)
    cols = frame.shape[0]
    gram = jnp.concatenate(
        [lined[:, cols * p : cols * (p + 1)] for p in range(cols // LON)], axis=0
    )
    put_frame(gram, rank, frame)
    lhs[...] = frame_rows(frame[...], rank)

    def push(level):
        return pltpu.make_async_copy(made.at[:, level], out.at[:, level], sems.at[level])

    def project(edge, base, level):
        for f in range(2):
            rows = [source[level, f] for source in (basis_inner, basis_edge, inner)]
            rows = jnp.concatenate(rows + [edge[level - base, f]], axis=0)
            both = jnp.dot(lhs[...], rows, preferred_element_type=F32)
            total = both[: rank * LON] + both[rank * LON :]
            made[:, level, f] = total.reshape(rank, LON, total.shape[1])

    pushes, base = [], 0
    for edge in edge_parts:
        for level in range(base, base + edge.shape[0]):
            project(edge, base, level)
            pushes.append(push(level))
            pushes[-1].start()
        base += edge.shape[0]
    for copy in pushes:
        copy.wait()


def final(grams, basis_inner, basis_edge, inner, edge_parts):
    levels, fields, height, lat = basis_inner.shape
    rank = height // HALF
    cols = rank + inner.shape[2] // HALF
    shape = (rank, levels, fields, LON, lat)
    return pl.pallas_call(
        final_kernel,
        in_specs=[pl.BlockSpec(memory_space=pltpu.VMEM)] * (4 + len(edge_parts)),
        out_specs=pl.BlockSpec(memory_space=pltpu.HBM),
        out_shape=jax.ShapeDtypeStruct(shape, F32),
        scratch_shapes=[
            pltpu.VMEM((cols, cols), F32),
            pltpu.VMEM((2 * rank * LON, cols * LON), BF16),
            pltpu.VMEM(shape, F32),
            pltpu.SemaphoreType.DMA((levels,)),
        ],
        compiler_params=pltpu.CompilerParams(vmem_limit_bytes=32 * MIB),
        name="frame_project",
    )(grams, basis_inner, basis_edge, inner, *edge_parts)


def on_device(winds, basis, ground):
    levels, lat = winds.shape[2], winds.shape[4]
    tiles = lax.axis_size("tile")
    devices = tiles * lax.axis_size("band")
    up_pairs = [(i, (i + 1) % tiles) for i in range(tiles)]
    down_pairs = [(j, i) for i, j in up_pairs]

    spans = spans_of(levels)
    halos, packed = [], ()
    for first, count in spans:
        up, down = packed = pack(winds, first, count, packed)
        halos.append((lax.ppermute(up, "tile", up_pairs), lax.ppermute(down, "tile", down_pairs)))

    cosine = jnp.cos((jnp.arange(lat, dtype=F32) + 0.5) * (jnp.pi / lat) - jnp.pi / 2)
    rows = jnp.stack([cosine, jnp.sqrt(cosine) / cosine / 12.0])
    rows = jnp.concatenate([rows, jnp.zeros((LON - 2, lat), F32)])
    ground = ground - lax.axis_index("band") * levels
    ground_edge = jnp.concatenate([ground[6:], ground[:2], ground[6:], ground[:2]])
    part, basis_edge, inner, basis_inner, gram = local(winds, basis, ground, rows)
    edge_parts = []
    for (first, count), halo in zip(spans, halos):
        edge, gram = edges(*halo, part, basis_edge, ground_edge, rows, gram, first, count, devices)
        edge_parts.append(edge)
    grams = lax.all_to_all(gram, ("band", "tile"), 0, 0)
    return final(grams, basis_inner, basis_edge, inner, edge_parts)


def solution(mesh):
    return jax.shard_map(
        on_device,
        mesh=mesh,
        in_specs=(
            P(None, None, "band", "tile", None),
            P(None, "band", None, "tile", None),
            P("tile", None),
        ),
        out_specs=P(None, "band", None, "tile", None),
        check_vma=False,
    )
```

```python
import functools

import jax
import jax.numpy as jnp
from jax import lax
from jax.experimental import pallas as pl
from jax.experimental.pallas import tpu as pltpu
from jax.sharding import PartitionSpec as P

ITERS = 4
HIGH = lax.Precision.HIGHEST
LON = 8
HALF = 4
TURN = 3
MIB = 1 << 20
LEAST_SHARE = 1e-6
AHEAD = 5
F32 = jnp.float32
BF16 = jnp.bfloat16


def rows_of(shape):
    return lax.broadcasted_iota(jnp.int32, shape, len(shape) - 2)


def lanes_of(shape):
    return lax.broadcasted_iota(jnp.int32, shape, len(shape) - 1)


def turn_of(levels):
    return TURN if levels % TURN == 0 else 1


def spans_of(levels):
    if levels % 2:
        return [(0, levels)]
    return [(0, levels // 2), (levels // 2, levels // 2)]


def whole_lanes(lat):
    return lat // 128 * 128


def pack_kernel(first, winds, *refs):
    up, down, held, sems = refs[-4:]
    fields, snaps = winds.shape[:2]
    turns, turn, lat = held.shape[0], held.shape[4], held.shape[6]
    main = whole_lanes(lat)
    pulls = []
    for n in range(turns):
        levels = pl.ds(first + n * turn, turn)
        for side, lon in enumerate((0, LON - 2)):
            pulls.append(
                pltpu.make_async_copy(
                    winds.at[:, :, levels, lon : lon + 2], held.at[n, side], sems.at[n, side]
                )
            )
            pulls[-1].start()
    odd = rows_of((LON, lat)) % 2 == 1
    for n in range(turns):
        pulls[2 * n].wait()
        pulls[2 * n + 1].wait()
        for f in range(fields):
            for g in range(snaps // 4):
                tails = ([], [])
                for i in range(turn):
                    low = [held[n, 0, f, 4 * g + t, i] for t in (0, 2, 1, 3)]
                    low = jnp.concatenate(low, axis=0)
                    low = jnp.where(odd, 8.0 * pltpu.roll(low, 1, 0), 0.0) - low
                    high = [held[n, 1, f, 4 * g + t, i] for t in (2, 0, 3, 1)]
                    high = jnp.concatenate(high, axis=0)
                    high = high - jnp.where(odd, 0.0, 8.0 * pltpu.roll(high, 7, 0))
                    for ref, tail, tile in ((down, tails[0], low), (up, tails[1], high)):
                        ref[f, n, g, :, i * main : (i + 1) * main] = tile[:, :main]
                        tail.append(tile[:, main:])
                for ref, tail in ((down, tails[0]), (up, tails[1])):
                    ref[f, n, g, :, turn * main :] = jnp.concatenate(tail, axis=1)


def pack(winds, first, count, after):
    fields, snaps, _, lon, lat = winds.shape
    turn = turn_of(count)
    turns = count // turn
    out = jax.ShapeDtypeStruct((fields, turns, snaps // 4, lon, turn * lat), F32)
    whole = pl.BlockSpec(memory_space=pltpu.VMEM)
    return pl.pallas_call(
        functools.partial(pack_kernel, first),
        in_specs=[pl.BlockSpec(memory_space=pltpu.HBM)]
        + [pl.BlockSpec(memory_space=pl.ANY)] * len(after),
        out_specs=[whole, whole],
        out_shape=[out, out],
        scratch_shapes=[
            pltpu.VMEM((turns, 2, fields, snaps, turn, 2, lat), F32),
            pltpu.SemaphoreType.DMA((turns, 2)),
        ],
        compiler_params=pltpu.CompilerParams(vmem_limit_bytes=52 * MIB),
        name="pack_halo",
    )(winds, *after)


def lat_diff(x):
    lat = x.shape[1]
    wide = pl.cdiv(lat + 2, 128) * 128
    x = jnp.concatenate([x, jnp.zeros((LON, wide - lat), F32)], axis=1)
    near = pltpu.roll(x, wide - 1, 1) - pltpu.roll(x, 1, 1)
    far = pltpu.roll(x, wide - 2, 1) - pltpu.roll(x, 2, 1)
    return (8.0 * near - far)[:, :lat]


def lon_diff_inside(x):
    row = rows_of(x.shape)
    out = jnp.where(row < 7, 8.0 * pltpu.roll(x, 7, 0), 0.0)
    out = out - jnp.where(row > 0, 8.0 * pltpu.roll(x, 1, 0), 0.0)
    out = out - jnp.where(row < 6, pltpu.roll(x, 6, 0), 0.0)
    return out + jnp.where(row > 1, pltpu.roll(x, 2, 0), 0.0)


def parted(planes):
    inner, edge = [], []
    for one, two in zip(planes[::2], planes[1::2]):
        top = rows_of(one.shape) < HALF
        one2, one6 = pltpu.roll(one, 2, 0), pltpu.roll(one, 6, 0)
        two2, two6 = pltpu.roll(two, 2, 0), pltpu.roll(two, 6, 0)
        inner.append(jnp.where(top, one6, two2))
        edge.append(jnp.where(top, one2, two6))
    return jnp.concatenate(inner, axis=0), jnp.concatenate(edge, axis=0)


def lon_trace(prod):
    rows, cols = prod.shape
    kept = jnp.where(rows_of(prod.shape) % HALF == lanes_of(prod.shape) % HALF, prod, 0.0)
    left = (lanes_of((rows // HALF, rows)) // HALF == rows_of((rows // HALF, rows))).astype(F32)
    right = (rows_of((cols, cols // HALF)) // HALF == lanes_of((cols, cols // HALF))).astype(F32)
    kept = jnp.dot(left, kept, precision=HIGH, preferred_element_type=F32)
    return jnp.dot(kept, right, precision=HIGH, preferred_element_type=F32)


def dot_lanes(a, b):
    return lax.dot_general(a, b, (((1,), (1,)), ((), ())), preferred_element_type=F32)


def local_kernel(
    winds, basis, ground, rows, edge, basis_edge, inner, basis_inner, gram, acc_inner, acc_edge
):
    level = pl.program_id(0)
    snaps, lat = winds.shape[1], winds.shape[4]
    rank = basis.shape[0]

    @pl.when(level == 0)
    def _():
        acc_inner[...] = jnp.zeros_like(acc_inner)
        acc_edge[...] = jnp.zeros_like(acc_edge)

    cosine = jnp.broadcast_to(rows[0:1, :], (LON, lat))
    scale = jnp.where(level < ground[...], jnp.broadcast_to(rows[1:2, :], (LON, lat)), 0.0)
    fields = ([], [])
    for t in range(snaps):
        east, north = winds[0, t, 0], winds[1, t, 0]
        fields[0].append((lon_diff_inside(north) - lat_diff(east * cosine)) * scale)
        fields[1].append((lon_diff_inside(east) + lat_diff(north * cosine)) * scale)
    for f in range(2):
        inside, outside = parted(fields[f])
        edge[0, f] = outside
        inside = inside.astype(BF16)
        inner[0, f] = inside
        b_inside, b_outside = parted([basis[c, 0, f].astype(F32) for c in range(rank)])
        b_inside, b_outside = b_inside.astype(BF16), b_outside.astype(BF16)
        basis_inner[0, f] = b_inside
        basis_edge[0, f] = b_outside
        block = jnp.concatenate([b_inside, inside], axis=0)
        acc_inner[...] += dot_lanes(block, block)
        acc_edge[...] += dot_lanes(b_outside, b_outside)

    @pl.when(level == pl.num_programs(0) - 1)
    def _():
        gram[...] = lon_trace(acc_inner[...])
        gram[0:rank, 0:rank] += lon_trace(acc_edge[...])


def local(winds, basis, ground, rows):
    fields, snaps, levels, lon, lat = winds.shape
    rank = basis.shape[0]
    cols = rank + snaps

    def each(height, dtype):
        block = pl.BlockSpec((1, fields, height, lat), lambda l: (l, 0, 0, 0))
        return block, jax.ShapeDtypeStruct((levels, fields, height, lat), dtype)

    outs = [
        each(snaps * HALF, F32),
        each(rank * HALF, BF16),
        each(snaps * HALF, BF16),
        each(rank * HALF, BF16),
        (
            pl.BlockSpec((cols, cols), lambda l: (0, 0)),
            jax.ShapeDtypeStruct((cols, cols), F32),
        ),
    ]
    return pl.pallas_call(
        local_kernel,
        grid=(levels,),
        in_specs=[
            pl.BlockSpec((fields, snaps, 1, lon, lat), lambda l: (0, 0, l, 0, 0)),
            pl.BlockSpec((rank, 1, fields, lon, lat), lambda l: (0, l, 0, 0, 0)),
            pl.BlockSpec((lon, lat), lambda l: (0, 0)),
            pl.BlockSpec((LON, lat), lambda l: (0, 0)),
        ],
        out_specs=[block for block, _ in outs],
        out_shape=[shape for _, shape in outs],
        scratch_shapes=[
            pltpu.VMEM((cols * HALF, cols * HALF), F32),
            pltpu.VMEM((rank * HALF, rank * HALF), F32),
        ],
        compiler_params=pltpu.CompilerParams(vmem_limit_bytes=40 * MIB),
        cost_estimate=pl.CostEstimate(
            flops=2 * 10**9, bytes_accessed=26 * 10**6, transcendentals=0
        ),
        name="local_stencil",
    )(winds, basis, ground, rows)


def edge_kernel(
    first, last, before, after, part, basis_edge, ground, rows, gram, snap, out, acc
):
    fields, height, lat = part.shape[1:]
    turns, groups = before.shape[1:3]
    turn = snap.shape[0] // turns
    main = whole_lanes(lat)
    rank = gram.shape[0] - height // HALF
    acc[...] = jnp.zeros_like(acc)
    row = rows_of((LON, lat))
    from_after = row % HALF < 2

    def tile(halo, n, f, g, i):
        start = turn * main + i * (lat - main)
        return jnp.concatenate(
            [
                halo[f, n, g, :, i * main : (i + 1) * main],
                halo[f, n, g, :, start : start + lat - main],
            ],
            axis=1,
        )

    for n in range(turns):
        for i in range(turn):
            here = n * turn + i
            level = first + here
            scale = jnp.where(level < ground[...], jnp.broadcast_to(rows[1:2, :], (LON, lat)), 0.0)
            for f in range(fields):
                tiles = []
                for g in range(groups):
                    high, low = tile(before, n, 1 - f, g, i), tile(after, n, 1 - f, g, i)
                    tiles.append(jnp.where(from_after, low, high))
                    tiles.append(
                        jnp.where(from_after, pltpu.roll(low, 6, 0), pltpu.roll(high, 2, 0))
                    )
                tiles = [
                    part[level, f, LON * p : LON * (p + 1)] + x * scale
                    for p, x in enumerate(tiles)
                ]
                block = jnp.concatenate(tiles, axis=0).astype(BF16)
                snap[here, f] = block
                both = jnp.concatenate([basis_edge[level, f], block], axis=0)
                acc[...] += dot_lanes(block, both)

    late = lon_trace(acc[...])
    cross = jnp.concatenate([jnp.zeros((rank, rank), F32), late[:, :rank].T], axis=1)
    total = gram[...] + jnp.concatenate([cross, late], axis=0)
    if not last:
        out[...] = total
        return
    cols = total.shape[0]
    lined = jnp.concatenate([total[LON * p : LON * (p + 1)] for p in range(cols // LON)], axis=1)
    out[...] = jnp.broadcast_to(lined[None], out.shape)


def edges(before, after, part, basis_edge, ground, rows, gram, first, count, devices):
    levels, fields, height, lat = part.shape
    cols = gram.shape[0]
    last = first + count == levels
    whole = pl.BlockSpec(memory_space=pltpu.VMEM)
    shape = (devices, LON, cols * cols // LON) if last else (cols, cols)
    return pl.pallas_call(
        functools.partial(edge_kernel, first, last),
        in_specs=[whole] * 7,
        out_specs=[whole, whole],
        out_shape=[
            jax.ShapeDtypeStruct((count, fields, height, lat), BF16),
            jax.ShapeDtypeStruct(shape, F32),
        ],
        scratch_shapes=[pltpu.VMEM((height, cols * HALF), F32)],
        compiler_params=pltpu.CompilerParams(vmem_limit_bytes=32 * MIB),
        cost_estimate=pl.CostEstimate(
            flops=10**8, bytes_accessed=6 * 10**6, transcendentals=0
        ),
        name="edge_gram",
    )(before, after, part, basis_edge, ground, rows, gram)


def spread_lane(block, j):
    return jnp.broadcast_to(block[:, j : j + 1], block.shape)


def down_sum(x):
    return jnp.sum(x, axis=0, keepdims=True)


def sweep(block, rank):
    lane = lanes_of(block.shape)
    whole = down_sum(block * block)
    ahead = [spread_lane(block, j) for j in range(AHEAD)]
    for j in range(rank):
        if j + AHEAD < rank:
            ahead.append(spread_lane(block, j + AHEAD))
        column = ahead.pop(0)
        inverse = 1.0 / down_sum(column * column)
        ahead = [x - column * (down_sum(column * x) * inverse) for x in ahead]
        part = jnp.where(lane[:1] > j, down_sum(column * block) * inverse, 0.0)
        block = block - column * part
    norm = down_sum(block * block)
    share = jnp.where(lane[:1] < rank, norm / whole, 1.0)
    return jnp.where(lane < rank, block / jnp.sqrt(norm), 0.0), share


def times(a, b):
    return jnp.dot(a, b, precision=HIGH, preferred_element_type=F32)


def unit(block, rank):
    scaled = block * lax.rsqrt(down_sum(block * block))
    return jnp.where(lanes_of(block.shape) < rank, scaled, 0.0)


def once_more(frame, rank):
    lane, row = lanes_of(frame.shape), rows_of(frame.shape)
    dots = lax.dot_general(
        frame, frame, (((0,), (0,)), ((), ())), precision=HIGH, preferred_element_type=F32
    )
    upper = jnp.where(row < lane, dots, 0.0)
    upper = upper + jnp.where(row == lane, 0.5 * (dots - 1.0), 0.0)
    return frame - times(frame, jnp.where(lane < rank, upper, 0.0))


def put_frame(gram, rank, frame_ref):
    frame, lost = None, jnp.zeros((1, gram.shape[1]), F32)
    for _ in range(ITERS // 2):
        frame = gram if frame is None else times(gram, frame)
        frame, share = sweep(times(gram, unit(frame, rank)), rank)
        lost = lost + jnp.where(share >= LEAST_SHARE, 0.0, 1.0)
    frame_ref[...] = once_more(frame, rank)

    @pl.when(jnp.sum(lost) > 0.5)
    def _():
        frame, _ = sweep(gram, rank)
        for _ in range(ITERS - 1):
            frame, _ = sweep(times(gram, frame), rank)
        frame_ref[...] = once_more(frame, rank)


def frame_rows(frame, rank):
    cols = frame.shape[0]
    wide = cols * LON
    near = rank * HALF

    def column(index):
        late = index >= 2 * near
        base = jnp.where(late, index - 2 * near, index)
        size = jnp.where(late, wide // 2 - near, near)
        second = base >= size
        base = jnp.where(second, base - size, base)
        lon = jnp.where(second, (index % HALF + 6) % LON, index % HALF + 2)
        return base // HALF + jnp.where(late, rank, 0), lon

    which, _ = column(lanes_of((cols, wide)))
    spread = (rows_of((cols, wide)) == which).astype(BF16)
    shape = (rank * LON, wide)
    _, lon = column(lanes_of(shape))
    kept = rows_of(shape) % LON == lon
    high = frame.astype(BF16)
    low = (frame - high.astype(F32)).astype(BF16)
    parts = []
    for part in (high, low):
        flat = lax.dot_general(
            part, spread, (((0,), (0,)), ((), ())), preferred_element_type=F32
        )[:rank]
        tall = jnp.broadcast_to(flat[:, None, :], (rank, LON, wide)).reshape(shape)
        parts.append(jnp.where(kept, tall, 0.0).astype(BF16))
    return jnp.concatenate(parts, axis=0)


def final_kernel(grams, basis_inner, basis_edge, inner, *refs):
    edge_parts, (out, frame, lhs, made, sems) = refs[:-5], refs[-5:]
    rank, levels = out.shape[:2]
    lined = jnp.sum(grams[...], axis=0)
    cols = frame.shape[0]
    gram = jnp.concatenate(
        [lined[:, cols * p : cols * (p + 1)] for p in range(cols // LON)], axis=0
    )
    put_frame(gram, rank, frame)
    lhs[...] = frame_rows(frame[...], rank)

    def push(level):
        return pltpu.make_async_copy(made.at[:, level], out.at[:, level], sems.at[level])

    def project(edge, base, level):
        for f in range(2):
            rows = [source[level, f] for source in (basis_inner, basis_edge, inner)]
            rows = jnp.concatenate(rows + [edge[level - base, f]], axis=0)
            both = jnp.dot(lhs[...], rows, preferred_element_type=F32)
            total = both[: rank * LON] + both[rank * LON :]
            made[:, level, f] = total.reshape(rank, LON, total.shape[1])

    pushes, base = [], 0
    for edge in edge_parts:
        for level in range(base, base + edge.shape[0]):
            project(edge, base, level)
            pushes.append(push(level))
            pushes[-1].start()
        base += edge.shape[0]
    for copy in pushes:
        copy.wait()


def final(grams, basis_inner, basis_edge, inner, edge_parts):
    levels, fields, height, lat = basis_inner.shape
    rank = height // HALF
    cols = rank + inner.shape[2] // HALF
    shape = (rank, levels, fields, LON, lat)
    return pl.pallas_call(
        final_kernel,
        in_specs=[pl.BlockSpec(memory_space=pltpu.VMEM)] * (4 + len(edge_parts)),
        out_specs=pl.BlockSpec(memory_space=pltpu.HBM),
        out_shape=jax.ShapeDtypeStruct(shape, F32),
        scratch_shapes=[
            pltpu.VMEM((cols, cols), F32),
            pltpu.VMEM((2 * rank * LON, cols * LON), BF16),
            pltpu.VMEM(shape, F32),
            pltpu.SemaphoreType.DMA((levels,)),
        ],
        compiler_params=pltpu.CompilerParams(vmem_limit_bytes=32 * MIB),
        name="frame_project",
    )(grams, basis_inner, basis_edge, inner, *edge_parts)


def on_device(winds, basis, ground):
    levels, lat = winds.shape[2], winds.shape[4]
    tiles = lax.axis_size("tile")
    devices = tiles * lax.axis_size("band")
    up_pairs = [(i, (i + 1) % tiles) for i in range(tiles)]
    down_pairs = [(j, i) for i, j in up_pairs]

    spans = spans_of(levels)
    halos, packed = [], ()
    for first, count in spans:
        up, down = packed = pack(winds, first, count, packed)
        halos.append((lax.ppermute(up, "tile", up_pairs), lax.ppermute(down, "tile", down_pairs)))

    cosine = jnp.cos((jnp.arange(lat, dtype=F32) + 0.5) * (jnp.pi / lat) - jnp.pi / 2)
    rows = jnp.stack([cosine, jnp.sqrt(cosine) / cosine / 12.0])
    rows = jnp.concatenate([rows, jnp.zeros((LON - 2, lat), F32)])
    ground = ground - lax.axis_index("band") * levels
    ground_edge = jnp.concatenate([ground[6:], ground[:2], ground[6:], ground[:2]])
    part, basis_edge, inner, basis_inner, gram = local(winds, basis, ground, rows)
    edge_parts = []
    for (first, count), halo in zip(spans, halos):
        edge, gram = edges(*halo, part, basis_edge, ground_edge, rows, gram, first, count, devices)
        edge_parts.append(edge)
    grams = lax.all_to_all(gram, ("band", "tile"), 0, 0)
    return final(grams, basis_inner, basis_edge, inner, edge_parts)


def solution(mesh):
    return jax.shard_map(
        on_device,
        mesh=mesh,
        in_specs=(
            P(None, None, "band", "tile", None),
            P(None, "band", None, "tile", None),
            P("tile", None),
        ),
        out_specs=P(None, "band", None, "tile", None),
        check_vma=False,
    )
```

```python
import functools

import jax
import jax.numpy as jnp
from jax import lax
from jax.experimental import pallas as pl
from jax.experimental.pallas import tpu as pltpu
from jax.sharding import PartitionSpec as P

ITERS = 4
HIGH = lax.Precision.HIGHEST
LON = 8
HALF = 4
TURN = 3
MIB = 1 << 20
LEAST_SHARE = 1e-6
AHEAD = 5
F32 = jnp.float32
BF16 = jnp.bfloat16


def rows_of(shape):
    return lax.broadcasted_iota(jnp.int32, shape, len(shape) - 2)


def lanes_of(shape):
    return lax.broadcasted_iota(jnp.int32, shape, len(shape) - 1)


def turn_of(levels):
    return TURN if levels % TURN == 0 else 1


def spans_of(levels):
    if levels % 2:
        return [(0, levels)]
    return [(0, levels // 2), (levels // 2, levels // 2)]


def whole_lanes(lat):
    return lat // 128 * 128


def odd_tile():
    return lax.axis_index("tile") % 2


def pack_kernel(first, winds, *refs):
    far, near, held, sems = refs[-4:]
    fields, snaps = winds.shape[:2]
    turns, turn, lat = held.shape[0], held.shape[4], held.shape[6]
    main = whole_lanes(lat)
    pulls = []
    for n in range(turns):
        levels = pl.ds(first + n * turn, turn)
        for side, lon in enumerate((0, LON - 2)):
            pulls.append(
                pltpu.make_async_copy(
                    winds.at[:, :, levels, lon : lon + 2], held.at[n, side], sems.at[n, side]
                )
            )
            pulls[-1].start()
    row = rows_of((LON, lat))
    odd = row % 2 == 1
    upward = jnp.zeros_like(row) + odd_tile() == 1
    for n in range(turns):
        pulls[2 * n].wait()
        pulls[2 * n + 1].wait()
        for f in range(fields):
            for g in range(snaps // 4):
                tails = ([], [])
                for i in range(turn):
                    low = [held[n, 0, f, 4 * g + t, i] for t in (0, 3, 1, 2)]
                    low = jnp.concatenate(low, axis=0)
                    low = jnp.where(odd, 8.0 * pltpu.roll(low, 1, 0), 0.0) - low
                    high = [held[n, 1, f, 4 * g + t, i] for t in (2, 0, 3, 1)]
                    high = jnp.concatenate(high, axis=0)
                    high = high - jnp.where(odd, 0.0, 8.0 * pltpu.roll(high, 7, 0))
                    pair = (jnp.where(upward, high, low), jnp.where(upward, low, high))
                    for ref, tail, tile in zip((far, near), tails, pair):
                        ref[f, n, g, :, i * main : (i + 1) * main] = tile[:, :main]
                        tail.append(tile[:, main:])
                for ref, tail in zip((far, near), tails):
                    ref[f, n, g, :, turn * main :] = jnp.concatenate(tail, axis=1)


def pack(winds, first, count, after):
    fields, snaps, _, lon, lat = winds.shape
    turn = turn_of(count)
    turns = count // turn
    out = jax.ShapeDtypeStruct((fields, turns, snaps // 4, lon, turn * lat), F32)
    whole = pl.BlockSpec(memory_space=pltpu.VMEM)
    return pl.pallas_call(
        functools.partial(pack_kernel, first),
        in_specs=[pl.BlockSpec(memory_space=pltpu.HBM)]
        + [pl.BlockSpec(memory_space=pl.ANY)] * len(after),
        out_specs=[whole, whole],
        out_shape=[out, out],
        scratch_shapes=[
            pltpu.VMEM((turns, 2, fields, snaps, turn, 2, lat), F32),
            pltpu.SemaphoreType.DMA((turns, 2)),
        ],
        compiler_params=pltpu.CompilerParams(vmem_limit_bytes=52 * MIB),
        name="pack_halo",
    )(winds, *after)


def lat_diff(x):
    lat = x.shape[1]
    wide = pl.cdiv(lat + 2, 128) * 128
    x = jnp.concatenate([x, jnp.zeros((LON, wide - lat), F32)], axis=1)
    near = pltpu.roll(x, wide - 1, 1) - pltpu.roll(x, 1, 1)
    far = pltpu.roll(x, wide - 2, 1) - pltpu.roll(x, 2, 1)
    return (8.0 * near - far)[:, :lat]


def lon_diff_inside(x):
    row = rows_of(x.shape)
    out = jnp.where(row < 7, 8.0 * pltpu.roll(x, 7, 0), 0.0)
    out = out - jnp.where(row > 0, 8.0 * pltpu.roll(x, 1, 0), 0.0)
    out = out - jnp.where(row < 6, pltpu.roll(x, 6, 0), 0.0)
    return out + jnp.where(row > 1, pltpu.roll(x, 2, 0), 0.0)


def parted(planes):
    inner, edge = [], []
    for one, two in zip(planes[::2], planes[1::2]):
        top = rows_of(one.shape) < HALF
        one2, one6 = pltpu.roll(one, 2, 0), pltpu.roll(one, 6, 0)
        two2, two6 = pltpu.roll(two, 2, 0), pltpu.roll(two, 6, 0)
        inner.append(jnp.where(top, one6, two2))
        edge.append(jnp.where(top, one2, two6))
    return jnp.concatenate(inner, axis=0), jnp.concatenate(edge, axis=0)


def lon_trace(prod):
    rows, cols = prod.shape
    kept = jnp.where(rows_of(prod.shape) % HALF == lanes_of(prod.shape) % HALF, prod, 0.0)
    left = (lanes_of((rows // HALF, rows)) // HALF == rows_of((rows // HALF, rows))).astype(F32)
    right = (rows_of((cols, cols // HALF)) // HALF == lanes_of((cols, cols // HALF))).astype(F32)
    kept = jnp.dot(left, kept, precision=HIGH, preferred_element_type=F32)
    return jnp.dot(kept, right, precision=HIGH, preferred_element_type=F32)


def dot_lanes(a, b):
    return lax.dot_general(a, b, (((1,), (1,)), ((), ())), preferred_element_type=F32)


def local_kernel(
    winds, basis, ground, rows, edge, basis_edge, inner, basis_inner, gram, acc_inner, acc_edge
):
    level = pl.program_id(0)
    snaps, lat = winds.shape[1], winds.shape[4]
    rank = basis.shape[0]

    @pl.when(level == 0)
    def _():
        acc_inner[...] = jnp.zeros_like(acc_inner)
        acc_edge[...] = jnp.zeros_like(acc_edge)

    cosine = jnp.broadcast_to(rows[0:1, :], (LON, lat))
    scale = jnp.where(level < ground[...], jnp.broadcast_to(rows[1:2, :], (LON, lat)), 0.0)
    fields = ([], [])
    for t in range(snaps):
        east, north = winds[0, t, 0], winds[1, t, 0]
        fields[0].append((lon_diff_inside(north) - lat_diff(east * cosine)) * scale)
        fields[1].append((lon_diff_inside(east) + lat_diff(north * cosine)) * scale)
    for f in range(2):
        inside, outside = parted(fields[f])
        edge[0, f] = outside
        inside = inside.astype(BF16)
        inner[0, f] = inside
        b_inside, b_outside = parted([basis[c, 0, f].astype(F32) for c in range(rank)])
        b_inside, b_outside = b_inside.astype(BF16), b_outside.astype(BF16)
        basis_inner[0, f] = b_inside
        basis_edge[0, f] = b_outside
        block = jnp.concatenate([b_inside, inside], axis=0)
        acc_inner[...] += dot_lanes(block, block)
        acc_edge[...] += dot_lanes(b_outside, b_outside)

    @pl.when(level == pl.num_programs(0) - 1)
    def _():
        gram[...] = lon_trace(acc_inner[...])
        gram[0:rank, 0:rank] += lon_trace(acc_edge[...])


def local(winds, basis, ground, rows):
    fields, snaps, levels, lon, lat = winds.shape
    rank = basis.shape[0]
    cols = rank + snaps

    def each(height, dtype):
        block = pl.BlockSpec((1, fields, height, lat), lambda l: (l, 0, 0, 0))
        return block, jax.ShapeDtypeStruct((levels, fields, height, lat), dtype)

    outs = [
        each(snaps * HALF, F32),
        each(rank * HALF, BF16),
        each(snaps * HALF, BF16),
        each(rank * HALF, BF16),
        (
            pl.BlockSpec((cols, cols), lambda l: (0, 0)),
            jax.ShapeDtypeStruct((cols, cols), F32),
        ),
    ]
    return pl.pallas_call(
        local_kernel,
        grid=(levels,),
        in_specs=[
            pl.BlockSpec((fields, snaps, 1, lon, lat), lambda l: (0, 0, l, 0, 0)),
            pl.BlockSpec((rank, 1, fields, lon, lat), lambda l: (0, l, 0, 0, 0)),
            pl.BlockSpec((lon, lat), lambda l: (0, 0)),
            pl.BlockSpec((LON, lat), lambda l: (0, 0)),
        ],
        out_specs=[block for block, _ in outs],
        out_shape=[shape for _, shape in outs],
        scratch_shapes=[
            pltpu.VMEM((cols * HALF, cols * HALF), F32),
            pltpu.VMEM((rank * HALF, rank * HALF), F32),
        ],
        compiler_params=pltpu.CompilerParams(vmem_limit_bytes=40 * MIB),
        cost_estimate=pl.CostEstimate(
            flops=2 * 10**9, bytes_accessed=26 * 10**6, transcendentals=0
        ),
        name="local_stencil",
    )(winds, basis, ground, rows)


def edge_kernel(
    first, last, far, near, part, basis_edge, ground, rows, gram, snap, out, acc
):
    fields, height, lat = part.shape[1:]
    turns, groups = far.shape[1:3]
    turn = snap.shape[0] // turns
    main = whole_lanes(lat)
    rank = gram.shape[0] - height // HALF
    acc[...] = jnp.zeros_like(acc)
    row = rows_of((LON, lat))
    from_near = row % HALF // 2 == odd_tile()

    def tile(halo, n, f, g, i):
        start = turn * main + i * (lat - main)
        return jnp.concatenate(
            [
                halo[f, n, g, :, i * main : (i + 1) * main],
                halo[f, n, g, :, start : start + lat - main],
            ],
            axis=1,
        )

    for n in range(turns):
        for i in range(turn):
            here = n * turn + i
            level = first + here
            scale = jnp.where(level < ground[...], jnp.broadcast_to(rows[1:2, :], (LON, lat)), 0.0)
            for f in range(fields):
                tiles = []
                for g in range(groups):
                    one, two = tile(far, n, 1 - f, g, i), tile(near, n, 1 - f, g, i)
                    tiles.append(jnp.where(from_near, two, one))
                    tiles.append(pltpu.roll(jnp.where(from_near, one, two), 2, 0))
                tiles = [
                    part[level, f, LON * p : LON * (p + 1)] + x * scale
                    for p, x in enumerate(tiles)
                ]
                block = jnp.concatenate(tiles, axis=0).astype(BF16)
                snap[here, f] = block
                both = jnp.concatenate([basis_edge[level, f], block], axis=0)
                acc[...] += dot_lanes(block, both)

    late = lon_trace(acc[...])
    cross = jnp.concatenate([jnp.zeros((rank, rank), F32), late[:, :rank].T], axis=1)
    total = gram[...] + jnp.concatenate([cross, late], axis=0)
    if not last:
        out[...] = total
        return
    cols = total.shape[0]
    lined = jnp.concatenate([total[LON * p : LON * (p + 1)] for p in range(cols // LON)], axis=1)
    out[...] = jnp.broadcast_to(lined[None], out.shape)


def edges(far, near, part, basis_edge, ground, rows, gram, first, count, devices):
    levels, fields, height, lat = part.shape
    cols = gram.shape[0]
    last = first + count == levels
    whole = pl.BlockSpec(memory_space=pltpu.VMEM)
    shape = (devices, LON, cols * cols // LON) if last else (cols, cols)
    return pl.pallas_call(
        functools.partial(edge_kernel, first, last),
        in_specs=[whole] * 7,
        out_specs=[whole, whole],
        out_shape=[
            jax.ShapeDtypeStruct((count, fields, height, lat), BF16),
            jax.ShapeDtypeStruct(shape, F32),
        ],
        scratch_shapes=[pltpu.VMEM((height, cols * HALF), F32)],
        compiler_params=pltpu.CompilerParams(vmem_limit_bytes=32 * MIB),
        cost_estimate=pl.CostEstimate(
            flops=10**8, bytes_accessed=6 * 10**6, transcendentals=0
        ),
        name="edge_gram",
    )(far, near, part, basis_edge, ground, rows, gram)


def spread_lane(block, j):
    return jnp.broadcast_to(block[:, j : j + 1], block.shape)


def down_sum(x):
    return jnp.sum(x, axis=0, keepdims=True)


def sweep(block, rank):
    lane = lanes_of(block.shape)
    whole = down_sum(block * block)
    ahead = [spread_lane(block, j) for j in range(AHEAD)]
    for j in range(rank):
        if j + AHEAD < rank:
            ahead.append(spread_lane(block, j + AHEAD))
        column = ahead.pop(0)
        inverse = 1.0 / down_sum(column * column)
        ahead = [x - column * (down_sum(column * x) * inverse) for x in ahead]
        part = jnp.where(lane[:1] > j, down_sum(column * block) * inverse, 0.0)
        block = block - column * part
    norm = down_sum(block * block)
    share = jnp.where(lane[:1] < rank, norm / whole, 1.0)
    return jnp.where(lane < rank, block / jnp.sqrt(norm), 0.0), share


def times(a, b):
    return jnp.dot(a, b, precision=HIGH, preferred_element_type=F32)


def unit(block, rank):
    scaled = block * lax.rsqrt(down_sum(block * block))
    return jnp.where(lanes_of(block.shape) < rank, scaled, 0.0)


def once_more(frame, rank):
    lane, row = lanes_of(frame.shape), rows_of(frame.shape)
    dots = lax.dot_general(
        frame, frame, (((0,), (0,)), ((), ())), precision=HIGH, preferred_element_type=F32
    )
    upper = jnp.where(row < lane, dots, 0.0)
    upper = upper + jnp.where(row == lane, 0.5 * (dots - 1.0), 0.0)
    return frame - times(frame, jnp.where(lane < rank, upper, 0.0))


def put_frame(gram, rank, frame_ref):
    frame, lost = None, jnp.zeros((1, gram.shape[1]), F32)
    for _ in range(ITERS // 2):
        frame = gram if frame is None else times(gram, frame)
        frame, share = sweep(times(gram, unit(frame, rank)), rank)
        lost = lost + jnp.where(share >= LEAST_SHARE, 0.0, 1.0)
    frame_ref[...] = once_more(frame, rank)

    @pl.when(jnp.sum(lost) > 0.5)
    def _():
        frame, _ = sweep(gram, rank)
        for _ in range(ITERS - 1):
            frame, _ = sweep(times(gram, frame), rank)
        frame_ref[...] = once_more(frame, rank)


def frame_rows(frame, rank):
    cols = frame.shape[0]
    wide = cols * LON
    near = rank * HALF

    def column(index):
        late = index >= 2 * near
        base = jnp.where(late, index - 2 * near, index)
        size = jnp.where(late, wide // 2 - near, near)
        second = base >= size
        base = jnp.where(second, base - size, base)
        lon = jnp.where(second, (index % HALF + 6) % LON, index % HALF + 2)
        return base // HALF + jnp.where(late, rank, 0), lon

    which, _ = column(lanes_of((cols, wide)))
    spread = (rows_of((cols, wide)) == which).astype(BF16)
    shape = (rank * LON, wide)
    _, lon = column(lanes_of(shape))
    kept = rows_of(shape) % LON == lon
    high = frame.astype(BF16)
    low = (frame - high.astype(F32)).astype(BF16)
    parts = []
    for part in (high, low):
        flat = lax.dot_general(
            part, spread, (((0,), (0,)), ((), ())), preferred_element_type=F32
        )[:rank]
        tall = jnp.broadcast_to(flat[:, None, :], (rank, LON, wide)).reshape(shape)
        parts.append(jnp.where(kept, tall, 0.0).astype(BF16))
    return jnp.concatenate(parts, axis=0)


def final_kernel(grams, basis_inner, basis_edge, inner, *refs):
    edge_parts, (out, frame, lhs, made, sems) = refs[:-5], refs[-5:]
    rank, levels = out.shape[:2]
    lined = jnp.sum(grams[...], axis=0)
    cols = frame.shape[0]
    gram = jnp.concatenate(
        [lined[:, cols * p : cols * (p + 1)] for p in range(cols // LON)], axis=0
    )
    put_frame(gram, rank, frame)
    lhs[...] = frame_rows(frame[...], rank)

    def push(level):
        return pltpu.make_async_copy(made.at[:, level], out.at[:, level], sems.at[level])

    def project(edge, base, level):
        for f in range(2):
            rows = [source[level, f] for source in (basis_inner, basis_edge, inner)]
            rows = jnp.concatenate(rows + [edge[level - base, f]], axis=0)
            both = jnp.dot(lhs[...], rows, preferred_element_type=F32)
            total = both[: rank * LON] + both[rank * LON :]
            made[:, level, f] = total.reshape(rank, LON, total.shape[1])

    pushes, base = [], 0
    for edge in edge_parts:
        for level in range(base, base + edge.shape[0]):
            project(edge, base, level)
            pushes.append(push(level))
            pushes[-1].start()
        base += edge.shape[0]
    for copy in pushes:
        copy.wait()


def final(grams, basis_inner, basis_edge, inner, edge_parts):
    levels, fields, height, lat = basis_inner.shape
    rank = height // HALF
    cols = rank + inner.shape[2] // HALF
    shape = (rank, levels, fields, LON, lat)
    return pl.pallas_call(
        final_kernel,
        in_specs=[pl.BlockSpec(memory_space=pltpu.VMEM)] * (4 + len(edge_parts)),
        out_specs=pl.BlockSpec(memory_space=pltpu.HBM),
        out_shape=jax.ShapeDtypeStruct(shape, F32),
        scratch_shapes=[
            pltpu.VMEM((cols, cols), F32),
            pltpu.VMEM((2 * rank * LON, cols * LON), BF16),
            pltpu.VMEM(shape, F32),
            pltpu.SemaphoreType.DMA((levels,)),
        ],
        compiler_params=pltpu.CompilerParams(vmem_limit_bytes=32 * MIB),
        name="frame_project",
    )(grams, basis_inner, basis_edge, inner, *edge_parts)


def on_device(winds, basis, ground):
    levels, lat = winds.shape[2], winds.shape[4]
    tiles = lax.axis_size("tile")
    devices = tiles * lax.axis_size("band")
    far_pairs = [(i, (i + 1 if i % 2 else i - 1) % tiles) for i in range(tiles)]
    near_pairs = [(i, i ^ 1) for i in range(tiles)]

    spans = spans_of(levels)
    halos, packed = [], ()
    for first, count in spans:
        far, near = packed = pack(winds, first, count, packed)
        halos.append((lax.ppermute(far, "tile", far_pairs), lax.ppermute(near, "tile", near_pairs)))

    cosine = jnp.cos((jnp.arange(lat, dtype=F32) + 0.5) * (jnp.pi / lat) - jnp.pi / 2)
    rows = jnp.stack([cosine, jnp.sqrt(cosine) / cosine / 12.0])
    rows = jnp.concatenate([rows, jnp.zeros((LON - 2, lat), F32)])
    ground = ground - lax.axis_index("band") * levels
    ground_edge = jnp.concatenate([ground[6:], ground[:2], ground[6:], ground[:2]])
    part, basis_edge, inner, basis_inner, gram = local(winds, basis, ground, rows)
    edge_parts = []
    for (first, count), halo in zip(spans, halos):
        edge, gram = edges(*halo, part, basis_edge, ground_edge, rows, gram, first, count, devices)
        edge_parts.append(edge)
    grams = lax.all_to_all(gram, ("band", "tile"), 0, 0)
    return final(grams, basis_inner, basis_edge, inner, edge_parts)


def solution(mesh):
    return jax.shard_map(
        on_device,
        mesh=mesh,
        in_specs=(
            P(None, None, "band", "tile", None),
            P(None, "band", None, "tile", None),
            P("tile", None),
        ),
        out_specs=P(None, "band", None, "tile", None),
        check_vma=False,
    )
```
